256 devices in a mesh: dom: 4 (over y), pencil: 64 (over x, z, core).
Axes of the slice: x: 4, y: 4, z: 8, core: 2. Of those that a mesh axis runs over, the one named last changes fastest.
Arguments:
- modes_now: float32 [4, 256, 256, 256], P('dom', 'pencil'), may hold values from -6 to 6
- modes_prev: float32 [4, 256, 256, 256], P('dom', 'pencil'), may hold values from -6 to 6
- extents: int32 [4, 2], replicated, may hold values from 128 to 256, as said below
- strips: int32 [8, 6], replicated, may hold values from 0 to 256, as said below
Outputs:
- modes_next: float32 [4, 256, 256, 256], P('dom', 'pencil')
- modes_last: float32 [4, 256, 256, 256], P('dom', 'pencil')
- pressure: float32 [4, 256, 256, 256], P('dom', None, 'pencil')
The draws below stay inside these ranges and needn't reach their ends.
Inputs may be any that keep to these rules, and one draw needn't show every extreme that they name: `extents`: row p holds partition p's lengths in cells along the first and the third dimension of its box; along the second dimension every partition has 256 cells. One partition has 256 along both, and two have 256 along the first. `strips`: row s is one strip (p, q, f, a, b, e): owner partition p, touching partition q with q != p, face f (0: p's face at third index 0 meets q's face at its last third index; 1: p's last face meets q's face at third index 0), start a in p and start b in q along the first dimension, extent e >= 1 with a + e at most p's first length and b + e at most q's. A strip covers all 256 cells of the second dimension. Some strip has e = 256.
All inputs are finite; a program needn't handle non-finite values.
Results may differ from the reference program's by a relative error of at most 0.0001.
Values sent between devices are 32-bit elements; how exact they have to be, the bound alone decides.
A program may use at most 64 MiB of HBM per device.

```python
import math
import jax
import jax.numpy as jnp
from jax import lax

M = 256
NSTRIP = 8
STEPS = 2
NPART = 4


def partition_layout(key):
    base_key = jax.random.fold_in(key, 7)
    key_length, key_pick = jax.random.split(base_key, 2)
    lengths = jax.random.randint(key_length, (NPART, 2), M // 2, M + 1)
    ordering = jax.random.permutation(key_pick, NPART)
    widest = ordering[0]
    second = ordering[1]
    group_index = jnp.arange(NPART, dtype=jnp.int32)
    full_first = (group_index == widest) | (group_index == second)
    first_len = jnp.where(full_first, M, lengths[:, 0])
    third_len = jnp.where(group_index == widest, M, lengths[:, 1])
    return (jnp.stack([first_len, third_len], axis=1).astype(jnp.int32), widest, second)


def draw_extents(key, part):
    lengths, widest, second = partition_layout(key)
    return lengths


def draw_strips(key, part):
    lengths, widest, second = partition_layout(key)
    strip_key = jax.random.fold_in(key, 11)
    strip_keys = jax.random.split(strip_key, 7)
    owners = jax.random.randint(strip_keys[0], (NSTRIP,), 0, NPART)
    others = (owners + jax.random.randint(strip_keys[1], (NSTRIP,), 1, NPART)) % NPART
    face_sides = jax.random.randint(strip_keys[2], (NSTRIP,), 0, 2)
    room_left = jnp.minimum(lengths[owners, 0], lengths[others, 0])
    extent = jax.random.randint(strip_keys[3], (NSTRIP,), 1, room_left + 1)
    start_own = jax.random.randint(strip_keys[4], (NSTRIP,), 0, lengths[owners, 0] - extent + 1)
    start_other = jax.random.randint(strip_keys[5], (NSTRIP,), 0, lengths[others, 0] - extent + 1)
    chosen_index = jax.random.randint(strip_keys[6], (), 0, NSTRIP)
    chosen_row = jnp.arange(NSTRIP, dtype=jnp.int32) == chosen_index
    owners = jnp.where(chosen_row, widest, owners)
    others = jnp.where(chosen_row, second, others)
    extent = jnp.where(chosen_row, M, extent)
    start_own = jnp.where(chosen_row, 0, start_own)
    start_other = jnp.where(chosen_row, 0, start_other)
    return jnp.stack([owners, others, face_sides, start_own, start_other, extent], axis=1).astype(jnp.int32)


def levels(rng, dims, shards, least, largest):
    def one(axis_at, parts):
        draws = jax.random.uniform(jax.random.fold_in(jax.random.fold_in(rng, 6), axis_at), (parts,), jnp.float32, least / len(shards), largest / len(shards))
        return jnp.repeat(jnp.exp(draws), dims[axis_at] // parts).reshape((-1,) + (1,) * (len(dims) - axis_at - 1))

    gain = one(*shards[0])
    for cut in shards[1:]:
        gain = gain * one(*cut)
    return gain


def scatter_about(stream_key, shape, width, reach, cuts=(), held_as=jnp.bfloat16):
    result = width * jax.random.normal(stream_key, shape, jnp.float32)
    if cuts:
        result = result * levels(stream_key, shape, cuts, -0.22, 0.18)
    return jnp.clip(result, -reach, reach).astype(held_as)


def setup_inputs(seed: int = 0) -> dict:
    key_of = jax.random.split(jax.random.key(seed), 5)
    modes_now = scatter_about(key_of[0], (NPART, M, M, M), 1.0, 6.0, ((0, 4), (1, 64)), jnp.float32)
    modes_prev = scatter_about(key_of[1], (NPART, M, M, M), 1.0, 6.0, ((0, 4), (1, 64)), jnp.float32)
    extents = draw_extents(jax.random.fold_in(key_of[4], 71), 0)
    strips = draw_strips(jax.random.fold_in(key_of[4], 71), 0)
    return dict(modes_now=modes_now, modes_prev=modes_prev, extents=extents, strips=strips)


COURANT = 0.5
PRECISE = lax.Precision.HIGHEST
COUPLING = ((1.5, -0.15, 2.0 / 180.0), (-0.15, 2.0 / 180.0, 0.0), (2.0 / 180.0, 0.0, 0.0))

def cosine_table(length, box_cells):
    length = jnp.asarray(length).astype(jnp.int32)
    wave_index = jnp.arange(box_cells, dtype=jnp.int32)[:, None]
    cell_index = jnp.arange(box_cells, dtype=jnp.int32)[None, :]
    phases = jnp.remainder(wave_index * (2 * cell_index + 1), 4 * length).astype(jnp.float32)
    float_length = length.astype(jnp.float32)
    scales = jnp.where(wave_index == 0, jnp.sqrt(1.0 / float_length), jnp.sqrt(2.0 / float_length))
    alive_mask = (wave_index < length) & (cell_index < length)
    values = scales * jnp.cos(phases * (math.pi / 2.0) / float_length)
    return jnp.where(alive_mask, values, 0.0).astype(jnp.float32)

def face_picker(length, box_cells):
    cell_index = jnp.arange(box_cells, dtype=jnp.int32)[:, None]
    slot_index = jnp.arange(6, dtype=jnp.int32)[None, :]
    target = jnp.where(slot_index < 3, slot_index, length - 1 - (slot_index - 3))
    return (cell_index == target).astype(jnp.float32)

def wave_factors(wave_rows, length_x, length_z, box_cells):
    wave_cols = jnp.arange(box_cells, dtype=jnp.int32)
    along_x = wave_rows.astype(jnp.float32) / length_x.astype(jnp.float32)
    along_y = wave_cols.astype(jnp.float32) / float(box_cells)
    along_z = wave_cols.astype(jnp.float32) / length_z.astype(jnp.float32)
    squared = along_x[:, None, None] ** 2 + along_y[None, :, None] ** 2 + along_z[None, None, :] ** 2
    angles = COURANT * math.pi * jnp.sqrt(squared)
    twice_cos = 2.0 * jnp.cos(angles)
    forcing_gain = jnp.sinc(angles / (2.0 * math.pi)) ** 2
    alive_mask = ((wave_rows < length_x)[:, None, None] & (wave_cols < length_z)[None, None, :]).astype(jnp.float32)
    return (twice_cos, forcing_gain, alive_mask)

def strip_maps(start_own, start_other, extent, box_cells):
    cell_index = jnp.arange(box_cells, dtype=jnp.int32)
    inside = (cell_index >= start_own) & (cell_index < start_own + extent)
    shifter = (cell_index[:, None] == cell_index[None, :] - start_own + start_other) & inside[None, :]
    return (shifter.astype(jnp.float32), inside.astype(jnp.float32))

def place_slots(values, face_side):
    depth = jnp.arange(3, dtype=jnp.int32)
    slot_index = jnp.arange(6, dtype=jnp.int32)
    spread = (slot_index[:, None] == face_side * 3 + depth[None, :]).astype(jnp.float32)
    coupling = jnp.asarray(COUPLING, dtype=jnp.float32)
    coupled = jnp.einsum('id,dyx->iyx', coupling, values, precision=PRECISE) * (COURANT * COURANT)
    return jnp.einsum('ci,iyx->cyx', spread, coupled, precision=PRECISE)

def other_part(other_faces, face_side, start_own, start_other, extent, box_cells):
    shifter, inside = strip_maps(start_own, start_other, extent, box_cells)
    depth = jnp.arange(3, dtype=jnp.int32)
    other_rows = jnp.take(other_faces, (1 - face_side) * 3 + depth, axis=0)
    aligned = jnp.einsum('dyx,xw->dyw', other_rows, shifter, precision=PRECISE)
    return place_slots(aligned, face_side)

def own_part(own_faces, face_side, start_own, start_other, extent, box_cells):
    shifter, inside = strip_maps(start_own, start_other, extent, box_cells)
    depth = jnp.arange(3, dtype=jnp.int32)
    own_rows = jnp.take(own_faces, face_side * 3 + depth, axis=0) * inside[None, None, :]
    return -place_slots(own_rows, face_side)

def inverse_full(mode_field, table_x, table_y, table_z):
    interim = jnp.einsum('abc,cz->abz', mode_field, table_z, precision=PRECISE)
    interim = jnp.einsum('abz,by->ayz', interim, table_y, precision=PRECISE)
    return jnp.einsum('ayz,ax->xyz', interim, table_x, precision=PRECISE)

def forward_full(forcing, picker, table_x, table_y, table_z):
    dense_force = jnp.einsum('cyx,zc->xyz', forcing, picker, precision=PRECISE)
    interim = jnp.einsum('xyz,ax->ayz', dense_force, table_x, precision=PRECISE)
    interim = jnp.einsum('ayz,by->abz', interim, table_y, precision=PRECISE)
    return jnp.einsum('abz,cz->abc', interim, table_z, precision=PRECISE)

def reference(modes_now, modes_prev, extents, strips):
    box_cells = modes_now.shape[1]
    table_y = cosine_table(box_cells, box_cells)
    current = [modes_now[index] for index in range(NPART)]
    previous = [modes_prev[index] for index in range(NPART)]
    for step_index in range(STEPS):
        face_list = []
        for partition in range(NPART):
            table_x = cosine_table(extents[partition, 0], box_cells)
            table_z = cosine_table(extents[partition, 1], box_cells)
            picker = face_picker(extents[partition, 1], box_cells)
            space_field = inverse_full(current[partition], table_x, table_y, table_z)
            face_list.append(jnp.einsum('xyz,zc->cyx', space_field, picker, precision=PRECISE))
        all_faces = jnp.stack(face_list)
        forcing_all = jnp.zeros((NPART, 6, box_cells, box_cells), jnp.float32)
        group_index = jnp.arange(NPART, dtype=jnp.int32)
        for strip_index in range(NSTRIP):
            owner_id = strips[strip_index, 0]
            other_id = strips[strip_index, 1]
            face_side = strips[strip_index, 2]
            start_own = strips[strip_index, 3]
            start_other = strips[strip_index, 4]
            extent = strips[strip_index, 5]
            strip_sum = other_part(all_faces[other_id], face_side, start_own, start_other, extent, box_cells)
            strip_sum = strip_sum + own_part(all_faces[owner_id], face_side, start_own, start_other, extent, box_cells)
            selector = (group_index == owner_id).astype(jnp.float32)
            forcing_all = forcing_all + selector[:, None, None, None] * strip_sum[None]
        updated = []
        for partition in range(NPART):
            length_x = extents[partition, 0]
            length_z = extents[partition, 1]
            table_x = cosine_table(length_x, box_cells)
            table_z = cosine_table(length_z, box_cells)
            picker = face_picker(length_z, box_cells)
            forced = forward_full(forcing_all[partition], picker, table_x, table_y, table_z)
            twice_cos, forcing_gain, alive_mask = wave_factors(jnp.arange(box_cells, dtype=jnp.int32), length_x, length_z, box_cells)
            updated.append((twice_cos * current[partition] - previous[partition] + forcing_gain * forced) * alive_mask)
        previous = current
        current = updated
    pressure_list = []
    for partition in range(NPART):
        table_x = cosine_table(extents[partition, 0], box_cells)
        table_z = cosine_table(extents[partition, 1], box_cells)
        pressure_list.append(inverse_full(current[partition], table_x, table_y, table_z))
    return (jnp.stack(current), jnp.stack(previous), jnp.stack(pressure_list))
```

```python
import functools
import math

import jax
import jax.numpy as jnp
from jax import lax
from jax.experimental import pallas as pl
from jax.experimental.pallas import tpu as pltpu
from jax.sharding import PartitionSpec as P

MESH = pl.DeviceIdType.MESH
COURANT = 0.5
PRECISE = lax.Precision.HIGHEST
CLOSE = lax.Precision.HIGH
COUPLING = ((1.5, -0.15, 2.0 / 180.0), (-0.15, 2.0 / 180.0, 0.0), (2.0 / 180.0, 0.0, 0.0))


def cosine_values(length, waves, cells):
    phases = jnp.remainder(waves * (2 * cells + 1), 4 * length).astype(jnp.float32)
    float_length = length.astype(jnp.float32)
    scales = jnp.where(waves == 0, jnp.sqrt(1.0 / float_length), jnp.sqrt(2.0 / float_length))
    values = scales * jnp.cos(phases * (math.pi / 2.0) / float_length)
    return jnp.where((waves < length) & (cells < length), values, 0.0)


def wave_factors(waves_x, waves_y, waves_z, length_x, length_z, box_cells):
    along_x = waves_x.astype(jnp.float32) / length_x.astype(jnp.float32)
    along_y = waves_y.astype(jnp.float32) / float(box_cells)
    along_z = waves_z.astype(jnp.float32) / length_z.astype(jnp.float32)
    angles = COURANT * math.pi * jnp.sqrt(along_x**2 + along_y**2 + along_z**2)
    live = ((waves_x < length_x) & (waves_z < length_z)).astype(jnp.float32)
    return 2.0 * jnp.cos(angles), jnp.sinc(angles / (2.0 * math.pi)) ** 2, live


def exchange_kernel(group, src, dst, own_sem, send_sem, recv_sem):
    me, size, device_of = group()
    own = pltpu.make_async_copy(src.at[me], dst.at[me], own_sem)
    own.start()
    barrier = pltpu.get_barrier_semaphore()

    def greet(step, carry):
        pl.semaphore_signal(barrier, inc=1, device_id=device_of(lax.rem(me + step, size)), device_id_type=MESH)
        return carry

    lax.fori_loop(1, size, greet, 0)
    pl.semaphore_wait(barrier, size - 1)

    def send(step, carry):
        peer = lax.rem(me + step, size)
        pltpu.make_async_remote_copy(
            src_ref=src.at[peer],
            dst_ref=dst.at[me],
            send_sem=send_sem,
            recv_sem=recv_sem,
            device_id=device_of(peer),
            device_id_type=MESH,
        ).start()
        return carry

    lax.fori_loop(1, size, send, 0)
    own.wait()
    pltpu.make_async_remote_copy(
        src_ref=src.at[pl.ds(0, size - 1)],
        dst_ref=dst.at[pl.ds(0, size - 1)],
        send_sem=send_sem,
        recv_sem=recv_sem,
        device_id=device_of(lax.rem(me + 1, size)),
        device_id_type=MESH,
    ).wait()


def exchange(values, group, collective_id, name):
    return pl.pallas_call(
        functools.partial(exchange_kernel, group),
        out_shape=jax.ShapeDtypeStruct(values.shape, values.dtype),
        in_specs=[pl.BlockSpec(memory_space=pltpu.VMEM)],
        out_specs=pl.BlockSpec(memory_space=pltpu.VMEM),
        scratch_shapes=[pltpu.SemaphoreType.DMA] * 3,
        compiler_params=pltpu.CompilerParams(
            has_side_effects=True, collective_id=collective_id, vmem_limit_bytes=32 << 20
        ),
        name=name,
    )(values)


def on_device(doms, pencils, modes_now, modes_prev, extents, strips):
    rows, box = modes_now.shape[1], modes_now.shape[2]
    everyone = doms * pencils

    def pencil_group():
        dom = lax.axis_index("dom")
        return lax.axis_index("pencil"), pencils, lambda peer: (dom, peer)

    def whole_group():
        me = lax.axis_index("dom") * pencils + lax.axis_index("pencil")
        return me, everyone, lambda peer: (peer // pencils, lax.rem(peer, pencils))

    dom, pencil = lax.axis_index("dom"), lax.axis_index("pencil")
    m0, m_old = modes_now[0], modes_prev[0]
    line = jnp.arange(box, dtype=jnp.int32)
    slots = jnp.arange(6, dtype=jnp.int32)
    lengths_x, lengths_z = extents[:, 0], extents[:, 1]
    length_x, length_z = extents[dom, 0], extents[dom, 1]
    slot_cells = jnp.where(slots < 3, slots, lengths_z[:, None] - 1 - (slots - 3))
    face_tables = cosine_values(lengths_z[:, None, None], line[None, :, None], slot_cells[:, None, :])
    face_table = face_tables[dom]
    x_tables = cosine_values(lengths_x[:, None, None], line[None, :, None], line[None, None, :])
    x_table = cosine_values(length_x, line[:, None], line[None, :])
    y_table = cosine_values(jnp.int32(box), line[:, None], line[None, :])
    z_table = cosine_values(length_z, line[:, None], line[None, :])

    twice_cos, gain, live = wave_factors(
        (pencil * rows + jnp.arange(rows, dtype=jnp.int32))[:, None, None],
        line[None, :, None],
        line[None, None, :],
        length_x,
        length_z,
        box,
    )
    free = live * (twice_cos * m0 - m_old)
    pushed = live * gain

    both = jnp.stack([m0, free])
    sent = jnp.einsum("uabc,cs->buas", both, face_table, precision=CLOSE).reshape(box, 1, 2 * rows * 6)
    sent = jnp.pad(sent, ((0, 0), (0, 0), (0, 128 - sent.shape[2])))
    got = exchange(sent, whole_group, 1, "faces_out")
    got = got[:, 0, : 2 * rows * 6].reshape(doms, pencils, 2, rows, 6)
    got = got.transpose(2, 0, 4, 1, 3).reshape(2, doms, 6, box)

    me = dom * pencils + pencil
    _, gain_b, live_b = wave_factors(
        line[None, :, None], me, line[None, None, :], lengths_x[:, None, None], lengths_z[:, None, None], box
    )
    pairs = (face_tables[:, :, :, None] * face_tables[:, :, None, :]).reshape(doms, box, 36)
    response = jnp.einsum("pac,pcw->paw", gain_b * live_b, pairs, precision=CLOSE).reshape(doms, box, 6, 6)

    owner, other, face, start, start_other, extent = (strips[:, i] for i in range(6))
    inside = (line >= start[:, None]) & (line < (start + extent)[:, None])
    shifter = ((line[None, :, None] == line[None, None, :] - start[:, None, None] + start_other[:, None, None]) & inside[:, None, :]).astype(jnp.float32)
    inside = inside.astype(jnp.float32)
    depth = jnp.arange(3, dtype=jnp.int32)
    dom_line = jnp.arange(doms, dtype=jnp.int32)

    def pick(dom_ids, sides):
        hit = (dom_ids[:, None, None, None] == dom_line[:, None]) & ((sides[:, None] * 3 + depth)[:, :, None, None] == slots)
        return hit.astype(jnp.float32)

    own_pick, other_pick = pick(owner, face), pick(other, 1 - face)
    coupling = jnp.asarray(COUPLING, dtype=jnp.float32) * (COURANT * COURANT)

    def force(face_modes):
        faces = jnp.einsum("psa,pax->psx", face_modes, x_tables, precision=CLOSE)
        theirs = jnp.einsum("edps,psx->edx", other_pick, faces, precision=PRECISE)
        ours = jnp.einsum("edps,psx->edx", own_pick, faces, precision=PRECISE)
        gap = jnp.einsum("edx,exw->edw", theirs, shifter, precision=PRECISE) - ours * inside[:, None, :]
        coupled = jnp.einsum("id,edx->eix", coupling, gap, precision=PRECISE)
        forcing = jnp.einsum("eips,eix->psx", own_pick, coupled, precision=PRECISE)
        return jnp.einsum("psx,pax->psa", forcing, x_tables, precision=CLOSE)

    force_one = force(got[0])
    force_two = force(got[1] + jnp.einsum("past,pta->psa", response, force_one, precision=PRECISE))

    back = jnp.stack([force_one, force_two]).reshape(2, doms, 6, pencils, rows)
    back = back.transpose(1, 3, 0, 4, 2).reshape(everyone, 1, 2 * rows * 6)
    back = jnp.pad(back, ((0, 0), (0, 0), (0, 128 - back.shape[2])))
    back = exchange(back, whole_group, 2, "forces_back")[:, 0, : 2 * rows * 6].reshape(box, 2, rows, 6)

    forced = jnp.einsum("buas,cs->uabc", back, face_table, precision=CLOSE)
    m1 = free + pushed * forced[0]
    m2 = live * (twice_cos * m1 - m0) + pushed * forced[1]

    interim = jnp.einsum("abc,cz->abz", m2, z_table, precision=CLOSE)
    interim = jnp.einsum("abz,by->ayz", interim, y_table, precision=CLOSE)
    interim = interim.reshape(rows, pencils, rows * box).transpose(1, 0, 2).reshape(pencils, rows * rows, box)
    pieces = exchange(interim, pencil_group, 3, "pressure_turn").reshape(box, rows, box)
    pressure = jnp.einsum("ayz,ax->xyz", pieces, x_table, precision=CLOSE)
    return (m2[None], m1[None], pressure[None])


def solution(mesh):
    return jax.shard_map(
        functools.partial(on_device, mesh.shape["dom"], mesh.shape["pencil"]),
        mesh=mesh,
        in_specs=(P("dom", "pencil", None, None), P("dom", "pencil", None, None), P(), P()),
        out_specs=(
            P("dom", "pencil", None, None),
            P("dom", "pencil", None, None),
            P("dom", None, "pencil", None),
        ),
        check_vma=False,
    )
```

```python
import functools
import math

import jax
import jax.numpy as jnp
from jax import lax
from jax.experimental import pallas as pl
from jax.experimental.pallas import tpu as pltpu
from jax.sharding import PartitionSpec as P

MESH = pl.DeviceIdType.MESH
F32, BF16, I32 = jnp.float32, jnp.bfloat16, jnp.int32
DOMS, PENCILS, BOX, ROWS = 4, 64, 256, 4
EVERYONE = DOMS * PENCILS
STRIPS = 8
HALF_PI = math.pi / 2.0
COUPLING = (1.5, -0.15, 2.0 / 180.0)
GAIN = (
    0.9999999999869928, -0.08333333316111119, 0.0027777774047159443, -4.960287119518586e-05,
    5.510286659542367e-07, -4.151822786228911e-09, 2.058914415718572e-11,
)
SINE = (
    1.5707963267681446, -0.6459640955780578, 0.07969260371703452, -0.004681657795344663,
    0.00016025469086571314, -3.431829236433259e-06,
)


def poly(coefs, t):
    value = jnp.full_like(t, coefs[-1])
    for coef in coefs[-2::-1]:
        value = value * t + coef
    return value


def split(value):
    high = value.astype(BF16)
    return high, (value - high.astype(F32)).astype(BF16)


def dot(left, right, left_dim, right_dim):
    return lax.dot_general(left, right, (((left_dim,), (right_dim,)), ((), ())), preferred_element_type=F32)


def dot3(left, right, left_dim=1, right_dim=0):
    return (
        dot(left[0], right[0], left_dim, right_dim)
        + dot(left[0], right[1], left_dim, right_dim)
        + dot(left[1], right[0], left_dim, right_dim)
    )


def dot_thin(value, right, right_dim):
    rows = value.shape[0]
    high = value.astype(BF16).astype(F32)
    left = jnp.concatenate([high, value - high], axis=0).astype(BF16)
    total = dot(left, right[0], 1, right_dim) + dot(left, right[1], 1, right_dim)
    return total[:rows] + total[rows:]


def iota(shape, dim):
    return lax.broadcasted_iota(I32, shape, dim)


def row_of(scalar):
    return jnp.full((1, BOX), scalar.astype(F32))


def cosines(length, waves, cells):
    width = max(waves.shape[1], cells.shape[1])
    long = jnp.full((1, width), length.astype(F32))
    inverse = 1.0 / long
    n = (waves * (2 * cells + 1)).astype(F32)
    turns = jnp.floor(n * (0.25 * inverse) + 0.5)
    u = 1.0 - jnp.abs(n - turns * (4.0 * long)) * inverse
    scale = jnp.where(waves == 0, jnp.sqrt(inverse), jnp.sqrt(2.0 * inverse))
    value = scale * u * poly(SINE, u * u)
    return jnp.where((waves < length) & (cells < length), value, 0.0)


def slot_cells(length_z, slots):
    return jnp.where(slots < 3, slots, length_z - 1 - (slots - 3))


def coupled_kernel(
    ext, strips, now, prev,
    one_out, two_out, pieces, xt_hi, xt_lo,
    m0, m_old, pushed, twice, free, sent, got, back, returned,
    tx_hi, tx_lo, response, edge_hi, edge_lo, tz_hi, tz_lo, ty_hi, ty_lo, mid_hi, mid_lo, turn,
    load_sem, own_sem, send_sem, recv_sem,
):
    dom, pencil = lax.axis_index("dom"), lax.axis_index("pencil")
    me = dom * PENCILS + pencil
    load_now = pltpu.make_async_copy(now, m0, load_sem.at[0])
    load_prev = pltpu.make_async_copy(prev, m_old, load_sem.at[1])
    load_now.start()
    load_prev.start()
    barrier = pltpu.get_barrier_semaphore()

    def device_of(step):
        peer = lax.rem(me + step, EVERYONE)
        return peer, (lax.div(peer, PENCILS), lax.rem(peer, PENCILS))

    def greet(first, count):
        for j in range(count):
            pl.semaphore_signal(barrier, inc=1, device_id=device_of(first + j)[1], device_id_type=MESH)

    def send_rows(source, target, leg, first, count):
        for j in range(count):
            peer, device = device_of(first + j)
            pltpu.make_async_remote_copy(
                src_ref=source.at[pl.ds(peer, 1)],
                dst_ref=target.at[pl.ds(me, 1)],
                send_sem=send_sem.at[leg],
                recv_sem=recv_sem.at[leg],
                device_id=device,
                device_id_type=MESH,
            ).start()

    def wait_rows(source, target, leg):
        pltpu.make_async_copy(source.at[pl.ds(me, 1)], target.at[pl.ds(me, 1)], own_sem.at[leg]).wait()
        pltpu.make_async_remote_copy(
            src_ref=source.at[pl.ds(0, EVERYONE - 1)],
            dst_ref=target.at[pl.ds(0, EVERYONE - 1)],
            send_sem=send_sem.at[leg],
            recv_sem=recv_sem.at[leg],
            device_id=device_of(1)[1],
            device_id_type=MESH,
        ).wait()

    length_x, length_z = ext[dom, 0], ext[dom, 1]

    lanes = iota((BOX, 128), 1)
    slots = lax.rem(lanes, 8)
    table = cosines(length_z, iota((BOX, 128), 0), slot_cells(length_z, slots))
    face_hi, face_lo = split(jnp.where(slots < 6, table, 0.0))
    waves_z = iota((1, BOX), 1)
    along_z = waves_z.astype(F32) * HALF_PI / row_of(length_z)
    along_z = along_z * along_z
    live_z = (waves_z < length_z).astype(F32)
    greet(1, 7)
    load_now.wait()
    load_prev.wait()
    block = 32
    groups = lax.div(iota((block, 128), 1), 8)

    def gather_faces(step, carry):
        at = pl.ds(pl.multiple_of(step * block, block), block)
        along_y = (iota((block, BOX), 0) + step * block).astype(F32) * (HALF_PI / BOX)
        along_y = along_y * along_y
        message = jnp.zeros((block, 128), F32)
        for a in range(ROWS):
            wave = pencil * ROWS + a
            along_x = row_of(wave) * HALF_PI / row_of(length_x)
            live = live_z * (jnp.full((1, BOX), wave) < length_x).astype(F32)
            t = along_y + (along_z + along_x * along_x)
            gain = poly(GAIN, t)
            twice_cos = 2.0 - t * gain
            here = m0[a, at, :]
            ahead = live * (twice_cos * here - m_old[a, at, :])
            pushed[a, at, :] = live * gain
            twice[a, at, :] = twice_cos
            free[a, at, :] = ahead
            for u, value in enumerate((here, ahead)):
                faces = dot3(split(value), (face_hi, face_lo))
                message = jnp.where(groups == u * ROWS + a, faces, message)
        sent[at, :] = message
        greet(8 + step * 31, 31)
        return carry

    lax.fori_loop(0, BOX // block, gather_faces, 0)
    pl.semaphore_wait(barrier, EVERYONE - 1)
    pltpu.make_async_copy(sent.at[pl.ds(me, 1)], got.at[pl.ds(me, 1)], own_sem.at[0]).start()
    send_rows(sent, got, 0, 1, 7)

    def x_tables(step, carry):
        send_rows(sent, got, 0, 8 + step * 10, 10)
        part, a = lax.div(step, ROWS), lax.rem(step, ROWS)
        at = pl.ds(pl.multiple_of(a * PENCILS, PENCILS), PENCILS)
        high, low = split(
            cosines(ext[part, 0], iota((PENCILS, BOX), 0) * ROWS + a, iota((PENCILS, BOX), 1))
        )
        tx_hi[part, at, :] = high
        tx_lo[part, at, :] = low
        return carry

    lax.fori_loop(0, DOMS * ROWS, x_tables, 0)

    def responses(step, carry):
        send_rows(sent, got, 0, 168 + step * 11, 11)
        part, half = lax.div(step, 2), lax.rem(step, 2)
        long_x, long_z = ext[part, 0], ext[part, 1]
        slot = iota((8, BOX), 0)
        rows = jnp.where(slot < 6, cosines(long_z, iota((8, BOX), 1), slot_cells(long_z, slot)), 0.0)
        pairs = jnp.concatenate([rows * rows[i : i + 1] for i in range(8)], axis=0)
        order = iota((128, BOX), 0) + half * 128
        waves = lax.rem(order, PENCILS) * ROWS + lax.div(order, PENCILS)
        along_x = waves.astype(F32) * HALF_PI / row_of(long_x)
        across = waves_z.astype(F32) * HALF_PI / row_of(long_z)
        along_y = row_of(me) * (HALF_PI / BOX)
        gain = poly(GAIN, along_x * along_x + (across * across + along_y * along_y))
        gain = jnp.where((waves < long_x) & (iota((128, BOX), 1) < long_z), gain, 0.0)
        response[part, half] = dot3(split(pairs), split(gain), 1, 1)
        return carry

    lax.fori_loop(0, DOMS * 2, responses, 0)

    def of_strip(strip_index, field):
        value = jnp.zeros_like(strip_index)
        for e in range(STRIPS):
            value = jnp.where(strip_index == e, strips[e, field], value)
        return value

    wide = iota((8 * STRIPS, 32), 0)
    index, depth = lax.div(wide, 8), lax.rem(wide, 8)
    column = iota((8 * STRIPS, 32), 1)
    part, slot = lax.div(column, 8), lax.rem(column, 8)
    face = of_strip(index, 2)

    def weights(parts, side):
        other = slot - 3 * side
        reach = depth + other
        value = jnp.where(reach == 0, 0.25 * COUPLING[0], jnp.where(reach == 1, 0.25 * COUPLING[1], 0.25 * COUPLING[2]))
        hit = (parts == part) & (other >= 0) & (other < 3) & (depth < 3) & (reach < 3)
        return jnp.where(hit, value, 0.0)

    takes = split(jnp.concatenate([weights(of_strip(index, 1), 1 - face), weights(of_strip(index, 0), face)], axis=0))
    tall = iota((32, 8 * STRIPS), 1)
    index, depth = lax.div(tall, 8), lax.rem(tall, 8)
    column = iota((32, 8 * STRIPS), 0)
    part, slot = lax.div(column, 8), lax.rem(column, 8)
    gives = (part == of_strip(index, 0)) & (slot == 3 * of_strip(index, 2) + depth) & (depth < 3)
    gives = jnp.where(gives, 1.0, 0.0).astype(BF16)
    index = lax.div(iota((8 * STRIPS, BOX), 0), 8)
    cells = iota((8 * STRIPS, BOX), 1)
    start = of_strip(index, 3)
    inside = (cells >= start) & (cells < start + of_strip(index, 5))

    def force(face_modes):
        faces = jnp.concatenate(
            [dot_thin(face_modes[p], (tx_hi[p], tx_lo[p]), 0) for p in range(DOMS)], axis=0
        )
        taken = dot3(takes, split(faces))
        shifted = [
            pltpu.roll(taken[8 * e : 8 * e + 8], lax.rem(strips[e, 3] - strips[e, 4] + BOX, BOX), 1)
            for e in range(STRIPS)
        ]
        gap = split(jnp.where(inside, jnp.concatenate(shifted, axis=0) - taken[8 * STRIPS :], 0.0))
        forcing = dot(gives, gap[0], 1, 0) + dot(gives, gap[1], 1, 0)
        return [dot_thin(forcing[8 * p : 8 * p + 8], (tx_hi[p], tx_lo[p]), 1) for p in range(DOMS)]

    wait_rows(sent, got, 0)
    first, second = [], []
    for pair in range(2):
        turned = got[128 * pair : 128 * pair + 128, :].T
        for p in range(2):
            for u, held in enumerate((first, second)):
                held.append(
                    jnp.concatenate(
                        [
                            turned[8 * (u * ROWS + a) : 8 * (u * ROWS + a) + 8, PENCILS * p : PENCILS * (p + 1)]
                            for a in range(ROWS)
                        ],
                        axis=1,
                    )
                )
    force_one = force(first)
    answered = []
    for p in range(DOMS):
        both = jnp.concatenate([response[p, 0], response[p, 1]], axis=1).reshape(8, 8, BOX)
        answered.append(second[p] + jnp.sum(both * force_one[p][None], axis=1))
    force_two = force(answered)
    for pair in range(2):
        rows = [
            jnp.concatenate(
                [forces[2 * pair + p][:, PENCILS * a : PENCILS * (a + 1)] for p in range(2)], axis=1
            )
            for forces in (force_one, force_two)
            for a in range(ROWS)
        ]
        rows.append(jnp.zeros((64, 128), F32))
        back[128 * pair : 128 * pair + 128, :] = jnp.concatenate(rows, axis=0).T
    pltpu.make_async_copy(back.at[pl.ds(me, 1)], returned.at[pl.ds(me, 1)], own_sem.at[1]).start()
    send_rows(back, returned, 1, 1, 15)

    def late_tables(step, carry):
        send_rows(back, returned, 1, 16 + step * 30, 30)
        at = pl.ds(pl.multiple_of(step * 32, 32), 32)
        near, far = iota((32, BOX), 0) + step * 32, iota((32, BOX), 1)
        tz_hi[at, :], tz_lo[at, :] = split(cosines(length_z, near, far))
        ty_hi[at, :], ty_lo[at, :] = split(cosines(jnp.int32(BOX), far, near))
        rows = iota((128, BOX), 0)
        cells = lax.rem(rows, 8)
        values = cosines(length_z, iota((128, BOX), 1), slot_cells(length_z, cells))
        values = jnp.where((cells < 6) & (lax.div(rows, 8) == step), values, 0.0)
        edge_hi[step], edge_lo[step] = split(values)
        return carry

    lax.fori_loop(0, 8, late_tables, 0)
    wait_rows(back, returned, 1)
    come = split(returned[...])
    top = iota((32, 8, BOX), 1) < 4
    own_turns = []
    for pair in range(2):
        planes = []
        for a in (2 * pair, 2 * pair + 1):
            wave = pencil * ROWS + a
            live = live_z * (jnp.full((1, BOX), wave) < length_x).astype(F32)
            for half in range(2):
                at = slice(128 * half, 128 * half + 128)
                left = (come[0][at], come[1][at])
                gain = pushed[a, at, :]
                m1 = free[a, at, :] + gain * dot3(left, (edge_hi[a], edge_lo[a]))
                one_out[a, at, :] = m1
                m2 = live * (twice[a, at, :] * m1 - m0[a, at, :]) + gain * dot3(
                    left, (edge_hi[ROWS + a], edge_lo[ROWS + a])
                )
                two_out[a, at, :] = m2
                middle = dot3(split(m2), (tz_hi[...], tz_lo[...]))
                mid_hi[at, :], mid_lo[at, :] = split(middle)
            plane = dot3((ty_hi[...], ty_lo[...]), (mid_hi[...], mid_lo[...]))
            planes.append(plane.reshape(32, 8, BOX))
        even = jnp.where(top, planes[0], pltpu.roll(planes[1], 4, 1))
        odd = jnp.where(top, pltpu.roll(planes[0], 4, 1), planes[1])
        for side in range(2):
            turn[side, pair, :, 0] = even[:, :, 128 * side : 128 * side + 128]
            turn[side, pair, :, 1] = odd[:, :, 128 * side : 128 * side + 128]
        own = pltpu.make_async_copy(
            turn.at[:, pair, lax.div(pencil, 2), lax.rem(pencil, 2)], pieces.at[:, pair, pencil], own_sem.at[2 + pair]
        )
        own.start()
        own_turns.append(own)

        def send_turn(step, carry):
            peer = lax.rem(pencil + step, PENCILS)
            pltpu.make_async_remote_copy(
                src_ref=turn.at[:, pair, lax.div(peer, 2), lax.rem(peer, 2)],
                dst_ref=pieces.at[:, pair, pencil],
                send_sem=send_sem.at[2 + pair],
                recv_sem=recv_sem.at[2 + pair],
                device_id=(dom, peer),
                device_id_type=MESH,
            ).start()
            return carry

        lax.fori_loop(1, PENCILS, send_turn, 0)

    def turned_tables(step, carry):
        at = pl.ds(pl.multiple_of(step * 32, 32), 32)
        order = iota((32, BOX), 1)
        waves = lax.rem(lax.div(order, 2), PENCILS) * ROWS + lax.div(order, 128) * 2 + lax.rem(order, 2)
        xt_hi[at, :], xt_lo[at, :] = split(cosines(length_x, waves, iota((32, BOX), 0) + step * 32))
        return carry

    lax.fori_loop(0, 8, turned_tables, 0)
    for pair in range(2):
        own_turns[pair].wait()
        pltpu.make_async_remote_copy(
            src_ref=pieces.at[:, pair, pl.ds(0, PENCILS - 1)],
            dst_ref=pieces.at[:, pair, pl.ds(0, PENCILS - 1)],
            send_sem=send_sem.at[2 + pair],
            recv_sem=recv_sem.at[2 + pair],
            device_id=(dom, lax.rem(pencil + 1, PENCILS)),
            device_id_type=MESH,
        ).wait()


def spread_kernel(pieces, xt_hi, xt_lo, one, two, one_out, two_out, pressure, sems):
    copies = [
        pltpu.make_async_copy(one, one_out, sems.at[0]),
        pltpu.make_async_copy(two, two_out, sems.at[1]),
    ]
    for copy in copies:
        copy.start()
    table = (xt_hi[...], xt_lo[...])
    for y in range(ROWS):
        for side in range(2):
            piece = pieces[pl.ds(side * BOX * ROWS + y, BOX, stride=ROWS), :]
            pressure[:, y, 128 * side : 128 * side + 128] = dot3(table, split(piece))
    for copy in copies:
        copy.wait()


def on_device(modes_now, modes_prev, extents, strips):
    vmem, smem, anywhere = (
        pl.BlockSpec(memory_space=space) for space in (pltpu.VMEM, pltpu.SMEM, pl.ANY)
    )
    field = jax.ShapeDtypeStruct((ROWS, BOX, BOX), F32)
    half_table = jax.ShapeDtypeStruct((BOX, BOX), BF16)
    one, two, pieces, xt_hi, xt_lo = pl.pallas_call(
        coupled_kernel,
        out_shape=(field, field, jax.ShapeDtypeStruct((2, 2, PENCILS, 8, 128), F32), half_table, half_table),
        in_specs=[smem, smem, anywhere, anywhere],
        out_specs=[vmem] * 5,
        scratch_shapes=[pltpu.VMEM((ROWS, BOX, BOX), F32)] * 5
        + [pltpu.VMEM((EVERYONE, 128), F32)] * 4
        + [pltpu.VMEM((DOMS, BOX, BOX), BF16)] * 2
        + [pltpu.VMEM((DOMS, 2, 64, 128), F32)]
        + [pltpu.VMEM((2 * ROWS, 128, BOX), BF16)] * 2
        + [pltpu.VMEM((BOX, BOX), BF16)] * 6
        + [pltpu.VMEM((2, 2, PENCILS // 2, 2, 8, 128), F32)]
        + [pltpu.SemaphoreType.DMA((2,))]
        + [pltpu.SemaphoreType.DMA((4,))] * 3,
        compiler_params=pltpu.CompilerParams(has_side_effects=True, collective_id=1, vmem_limit_bytes=44 << 20),
        name="coupled",
    )(extents, strips, modes_now[0], modes_prev[0])
    one, two, pressure = pl.pallas_call(
        spread_kernel,
        out_shape=(field, field, jax.ShapeDtypeStruct((BOX, ROWS, BOX), F32)),
        in_specs=[vmem] * 5,
        out_specs=[anywhere, anywhere, vmem],
        scratch_shapes=[pltpu.SemaphoreType.DMA((2,))],
        compiler_params=pltpu.CompilerParams(vmem_limit_bytes=24 << 20),
        name="spread",
    )(pieces.reshape(2 * BOX * ROWS, 128), xt_hi, xt_lo, one, two)
    return (two[None], one[None], pressure[None])


def solution(mesh):
    return jax.shard_map(
        on_device,
        mesh=mesh,
        in_specs=(P("dom", "pencil", None, None), P("dom", "pencil", None, None), P(), P()),
        out_specs=(
            P("dom", "pencil", None, None),
            P("dom", "pencil", None, None),
            P("dom", None, "pencil", None),
        ),
        check_vma=False,
    )
```

```python
import functools
import math

import jax
import jax.numpy as jnp
from jax import lax
from jax.experimental import pallas as pl
from jax.experimental.pallas import tpu as pltpu
from jax.sharding import PartitionSpec as P

MESH = pl.DeviceIdType.MESH
F32, BF16, I32 = jnp.float32, jnp.bfloat16, jnp.int32
DOMS, PENCILS, BOX, ROWS = 4, 64, 256, 4
EVERYONE = DOMS * PENCILS
STRIPS = 8
HALF_PI = math.pi / 2.0
COUPLING = (1.5, -0.15, 2.0 / 180.0)
GAIN = (
    0.9999999999869928, -0.08333333316111119, 0.0027777774047159443, -4.960287119518586e-05,
    5.510286659542367e-07, -4.151822786228911e-09, 2.058914415718572e-11,
)
PUSHED_GAIN = (
    1.9999999838483329, -1.1666663858596251, 0.17222142001421806, -0.012598331258825314,
    0.0005628010719150018, -1.6955597515164814e-05, 3.5301674212625207e-07, -4.241805096348839e-09,
)
MID = math.pi**2 / 8.0
BULK = (1, 2, 16, 0)
SINE = (
    1.5707963267681446, -0.6459640955780578, 0.07969260371703452, -0.004681657795344663,
    0.00016025469086571314, -3.431829236433259e-06,
)


def poly(coefs, t):
    value = jnp.full_like(t, coefs[-1])
    for coef in coefs[-2::-1]:
        value = value * t + coef
    return value


def split(value):
    high = value.astype(BF16)
    return high, (value - high.astype(F32)).astype(BF16)


def dot(left, right, left_dim, right_dim):
    return lax.dot_general(left, right, (((left_dim,), (right_dim,)), ((), ())), preferred_element_type=F32)


def dot3(left, right, left_dim=1, right_dim=0):
    return (
        dot(left[0], right[0], left_dim, right_dim)
        + dot(left[0], right[1], left_dim, right_dim)
        + dot(left[1], right[0], left_dim, right_dim)
    )


def dot_thin(value, right, right_dim):
    rows = value.shape[0]
    high = value.astype(BF16).astype(F32)
    left = jnp.concatenate([high, value - high], axis=0).astype(BF16)
    total = dot(left, right[0], 1, right_dim) + dot(left, right[1], 1, right_dim)
    return total[:rows] + total[rows:]


def iota(shape, dim):
    return lax.broadcasted_iota(I32, shape, dim)


def row_of(scalar):
    return jnp.full((1, BOX), scalar.astype(F32))


def cosines(length, waves, cells):
    width = max(waves.shape[1], cells.shape[1])
    long = jnp.full((1, width), length.astype(F32))
    inverse = 1.0 / long
    n = (waves * (2 * cells + 1)).astype(F32)
    turns = jnp.floor(n * (0.25 * inverse) + 0.5)
    u = 1.0 - jnp.abs(n - turns * (4.0 * long)) * inverse
    scale = jnp.where(waves == 0, jnp.sqrt(inverse), jnp.sqrt(2.0 * inverse))
    value = scale * u * poly(SINE, u * u)
    return jnp.where((waves < length) & (cells < length), value, 0.0)


def slot_cells(length_z, slots):
    return jnp.where(slots < 3, slots, length_z - 1 - (slots - 3))


def coupled_kernel(
    ext_in, strips_in, now, prev,
    one_out, two_out, pieces, late, xt_hi, xt_lo, zt_hi, zt_lo,
    m0, m_old, pushed, twice, free, sent, got, back, returned,
    tx_hi, tx_lo, response, edge_hi, edge_lo, tz_hi, tz_lo, ty_hi, ty_lo, mid_hi, mid_lo, turn, lift, late_turn, ext, strips,
    load_sem, own_sem, send_sem, recv_sem,
):
    dom, pencil = lax.axis_index("dom"), lax.axis_index("pencil")
    me = dom * PENCILS + pencil
    load_now = pltpu.make_async_copy(now, m0, load_sem.at[0])
    load_prev = pltpu.make_async_copy(prev, m_old, load_sem.at[1])
    small_loads = [
        pltpu.make_async_copy(ext_in, ext, load_sem.at[2]),
        pltpu.make_async_copy(strips_in, strips, load_sem.at[3]),
    ]
    for load in (*small_loads, load_now, load_prev):
        load.start()
    barrier = pltpu.get_barrier_semaphore()

    doms = [lax.rem(dom + d, DOMS) for d in range(DOMS)]

    def devices(shift, own_pencil=False):
        around = pencil if own_pencil else lax.rem(pencil + shift, PENCILS)
        return [(d * PENCILS + around, (d, around)) for d in (doms[1:] if own_pencil else doms)]

    def greet(first, count):
        for shift in range(count):
            for _, device in devices(first + shift):
                pl.semaphore_signal(barrier, inc=1, device_id=device, device_id_type=MESH)

    def greet_own():
        for _, device in devices(0, True):
            pl.semaphore_signal(barrier, inc=1, device_id=device, device_id_type=MESH)

    def send_row(source, target, leg, peer, device):
        pltpu.make_async_remote_copy(
            src_ref=source.at[pl.ds(peer, 1)],
            dst_ref=target.at[pl.ds(me, 1)],
            send_sem=send_sem.at[leg],
            recv_sem=recv_sem.at[leg],
            device_id=device,
            device_id_type=MESH,
        ).start()

    def send_rows(source, target, leg, first, count):
        for shift in range(count):
            for peer, device in devices(first + shift):
                send_row(source, target, leg, peer, device)

    def send_own(source, target, leg):
        for peer, device in devices(0, True):
            send_row(source, target, leg, peer, device)

    def send_turn(source, target, leg, first, count):
        for j in range(count):
            peer = lax.rem(pencil + first + j, PENCILS)
            pltpu.make_async_remote_copy(
                src_ref=source(peer),
                dst_ref=target(pencil),
                send_sem=send_sem.at[leg],
                recv_sem=recv_sem.at[leg],
                device_id=(dom, peer),
                device_id_type=MESH,
            ).start()

    def turn_of(peer):
        return turn.at[:, :, lax.div(peer, 2), lax.rem(peer, 2)]

    def pieces_of(peer):
        return pieces.at[:, :, peer]

    def late_turn_of(peer):
        return late_turn.at[lax.div(peer, 2), lax.rem(peer, 2)]

    def late_of(peer):
        return late.at[peer]

    def wait_rows(source, target, leg):
        pltpu.make_async_copy(source.at[pl.ds(me, 1)], target.at[pl.ds(me, 1)], own_sem.at[leg]).wait()
        pltpu.make_async_remote_copy(
            src_ref=source.at[pl.ds(0, EVERYONE - 1)],
            dst_ref=target.at[pl.ds(0, EVERYONE - 1)],
            send_sem=send_sem.at[leg],
            recv_sem=recv_sem.at[leg],
            device_id=(doms[1], pencil),
            device_id_type=MESH,
        ).wait()

    greet_own()
    greet(1, 7)
    for load in small_loads:
        load.wait()
    length_x, length_z = ext[0, dom], ext[1, dom]

    lanes = iota((BOX, 128), 1)
    slots = lax.rem(lanes, 8)
    table = cosines(length_z, iota((BOX, 128), 0), slot_cells(length_z, slots))
    face_hi, face_lo = split(jnp.where(slots < 6, table, 0.0))
    waves_z = iota((1, BOX), 1)
    along_z = waves_z.astype(F32) * HALF_PI / row_of(length_z)
    along_z = along_z * along_z
    live_z = (waves_z < length_z).astype(F32)
    def first_tables(step, carry):
        at = pl.ds(pl.multiple_of(step * 32, 32), 32)
        near, far = iota((32, BOX), 0) + step * 32, iota((32, BOX), 1)
        tz_hi[at, :], tz_lo[at, :] = split(cosines(length_z, near, far))
        ty_hi[at, :], ty_lo[at, :] = split(cosines(jnp.int32(BOX), far, near))
        greet(8 + step * 3, 3)
        return carry

    lax.fori_loop(0, 8, first_tables, 0)
    load_now.wait()
    load_prev.wait()
    block = 32
    groups = lax.div(iota((block, 128), 1), 8)

    def gather_faces(step, carry):
        at = pl.ds(pl.multiple_of(step * block, block), block)
        along_y = (iota((block, BOX), 0) + step * block).astype(F32) * (HALF_PI / BOX)
        along_y = along_y * along_y
        message = jnp.zeros((block, 128), F32)
        for a in range(ROWS):
            wave = pencil * ROWS + a
            along_x = row_of(wave) * HALF_PI / row_of(length_x)
            live = live_z * (jnp.full((1, BOX), wave) < length_x).astype(F32)
            t = along_y + (along_z + along_x * along_x)
            gain = poly(GAIN, t)
            twice_cos = 2.0 - t * gain
            here = m0[a, at, :]
            ahead = live * (twice_cos * here - m_old[a, at, :])
            pushed[a, at, :] = live * gain
            twice[a, at, :] = twice_cos
            free[a, at, :] = ahead
            base = live * (twice_cos * ahead - here)
            mid_hi[a, at, :], mid_lo[a, at, :] = split(dot3(split(base), (tz_hi[...], tz_lo[...])))
            for u, value in enumerate((here, ahead)):
                faces = dot3(split(value), (face_hi, face_lo))
                message = jnp.where(groups == u * ROWS + a, faces, message)
        sent[at, :] = message
        greet(32 + step * 4, 4)
        return carry

    lax.fori_loop(0, BOX // block, gather_faces, 0)
    top = iota((32, 8, BOX), 1) < 4

    def weave(first, second):
        upper = top[:, :, : first.shape[2]]
        even = jnp.where(upper, first, pltpu.roll(second, 4, 1))
        return even, jnp.where(upper, pltpu.roll(first, 4, 1), second)

    for pair in range(2):
        planes = [
            dot3((ty_hi[...], ty_lo[...]), (mid_hi[a], mid_lo[a])).reshape(32, 8, BOX)
            for a in (2 * pair, 2 * pair + 1)
        ]
        for parity, woven in enumerate(weave(*planes)):
            for side in range(2):
                turn[side, pair, :, parity] = woven[:, :, 128 * side : 128 * side + 128]
    pl.semaphore_wait(barrier, EVERYONE - 1)
    pltpu.make_async_copy(sent.at[pl.ds(me, 1)], got.at[pl.ds(me, 1)], own_sem.at[0]).start()
    send_own(sent, got, 0)
    send_rows(sent, got, 0, 1, 7)
    own_turn = pltpu.make_async_copy(turn_of(pencil), pieces_of(pencil), own_sem.at[2])
    own_turn.start()
    bulk_one, bulk_two, bulk_three, bulk_four = BULK
    bulk_after_one = 1 + DOMS * ROWS * bulk_one
    bulk_after_two = bulk_after_one + DOMS * 2 * bulk_two
    bulk_after_three = bulk_after_two + bulk_three
    bulk_after_four = bulk_after_three + 8 * bulk_four

    def x_tables(step, carry):
        send_rows(sent, got, 0, 8 + step * 3, 3)
        send_turn(turn_of, pieces_of, 2, 1 + step * bulk_one, bulk_one)
        part, a = lax.div(step, ROWS), lax.rem(step, ROWS)
        at = pl.ds(pl.multiple_of(a * PENCILS, PENCILS), PENCILS)
        high, low = split(
            cosines(ext[0, part], iota((PENCILS, BOX), 0) * ROWS + a, iota((PENCILS, BOX), 1))
        )
        tx_hi[part, at, :] = high
        tx_lo[part, at, :] = low
        return carry

    lax.fori_loop(0, DOMS * ROWS, x_tables, 0)

    def responses(step, carry):
        send_rows(sent, got, 0, 56 + step, 1)
        send_turn(turn_of, pieces_of, 2, bulk_after_one + step * bulk_two, bulk_two)
        part, half = lax.div(step, 2), lax.rem(step, 2)
        long_x, long_z = ext[0, part], ext[1, part]
        slot = iota((8, BOX), 0)
        rows = jnp.where(slot < 6, cosines(long_z, iota((8, BOX), 1), slot_cells(long_z, slot)), 0.0)
        pairs = jnp.concatenate([rows * rows[i : i + 1] for i in range(8)], axis=0)
        order = iota((128, BOX), 0) + half * 128
        waves = lax.rem(order, PENCILS) * ROWS + lax.div(order, PENCILS)
        along_x = waves.astype(F32) * HALF_PI / row_of(long_x)
        across = waves_z.astype(F32) * HALF_PI / row_of(long_z)
        along_y = row_of(me) * (HALF_PI / BOX)
        gain = poly(GAIN, along_x * along_x + (across * across + along_y * along_y))
        gain = jnp.where((waves < long_x) & (iota((128, BOX), 1) < long_z), gain, 0.0)
        response[part, half] = dot3(split(pairs), split(gain), 1, 1)
        return carry

    lax.fori_loop(0, DOMS * 2, responses, 0)

    def of_strip(strip_index, field):
        value = jnp.zeros_like(strip_index)
        for e in range(STRIPS):
            value = jnp.where(strip_index == e, strips[e, field], value)
        return value

    wide = iota((8 * STRIPS, 32), 0)
    index, depth = lax.div(wide, 8), lax.rem(wide, 8)
    column = iota((8 * STRIPS, 32), 1)
    part, slot = lax.div(column, 8), lax.rem(column, 8)
    face = of_strip(index, 2)

    def weights(parts, side):
        other = slot - 3 * side
        reach = depth + other
        value = jnp.where(reach == 0, 0.25 * COUPLING[0], jnp.where(reach == 1, 0.25 * COUPLING[1], 0.25 * COUPLING[2]))
        hit = (parts == part) & (other >= 0) & (other < 3) & (depth < 3) & (reach < 3)
        return jnp.where(hit, value, 0.0)

    takes = split(jnp.concatenate([weights(of_strip(index, 1), 1 - face), weights(of_strip(index, 0), face)], axis=0))
    tall = iota((32, 8 * STRIPS), 1)
    index, depth = lax.div(tall, 8), lax.rem(tall, 8)
    column = iota((32, 8 * STRIPS), 0)
    part, slot = lax.div(column, 8), lax.rem(column, 8)
    gives = (part == of_strip(index, 0)) & (slot == 3 * of_strip(index, 2) + depth) & (depth < 3)
    gives = jnp.where(gives, 1.0, 0.0).astype(BF16)
    index = lax.div(iota((8 * STRIPS, BOX), 0), 8)
    cells = iota((8 * STRIPS, BOX), 1)
    start = of_strip(index, 3)
    inside = (cells >= start) & (cells < start + of_strip(index, 5))

    def force(face_modes):
        faces = jnp.concatenate(
            [dot_thin(face_modes[p], (tx_hi[p], tx_lo[p]), 0) for p in range(DOMS)], axis=0
        )
        taken = dot3(takes, split(faces))
        shifted = [
            pltpu.roll(taken[8 * e : 8 * e + 8], lax.rem(strips[e, 3] - strips[e, 4] + BOX, BOX), 1)
            for e in range(STRIPS)
        ]
        gap = split(jnp.where(inside, jnp.concatenate(shifted, axis=0) - taken[8 * STRIPS :], 0.0))
        forcing = dot(gives, gap[0], 1, 0) + dot(gives, gap[1], 1, 0)
        return [dot_thin(forcing[8 * p : 8 * p + 8], (tx_hi[p], tx_lo[p]), 1) for p in range(DOMS)]

    wait_rows(sent, got, 0)
    send_turn(turn_of, pieces_of, 2, bulk_after_two, bulk_three)
    first, second = [], []
    for pair in range(2):
        turned = got[128 * pair : 128 * pair + 128, :].T
        for p in range(2):
            for u, held in enumerate((first, second)):
                held.append(
                    jnp.concatenate(
                        [
                            turned[8 * (u * ROWS + a) : 8 * (u * ROWS + a) + 8, PENCILS * p : PENCILS * (p + 1)]
                            for a in range(ROWS)
                        ],
                        axis=1,
                    )
                )
    force_one = force(first)
    answered = []
    for p in range(DOMS):
        both = jnp.concatenate([response[p, 0], response[p, 1]], axis=1).reshape(8, 8, BOX)
        answered.append(second[p] + jnp.sum(both * force_one[p][None], axis=1))
    force_two = force(answered)
    for pair in range(2):
        rows = [
            jnp.concatenate(
                [forces[2 * pair + p][:, PENCILS * a : PENCILS * (a + 1)] for p in range(2)], axis=1
            )
            for forces in (force_one, force_two)
            for a in range(ROWS)
        ]
        rows.append(jnp.zeros((64, 128), F32))
        back[128 * pair : 128 * pair + 128, :] = jnp.concatenate(rows, axis=0).T
    pltpu.make_async_copy(back.at[pl.ds(me, 1)], returned.at[pl.ds(me, 1)], own_sem.at[1]).start()
    send_own(back, returned, 1)
    send_rows(back, returned, 1, 1, 7)

    chunk = iota((1, 128), 1)
    later, power = lax.div(chunk, 64), lax.rem(lax.div(chunk, 8), 8)
    rows_of = []
    for m in range(8):
        row = jnp.zeros((1, 128), F32)
        for u, coefs in enumerate((PUSHED_GAIN, GAIN)):
            for j in range(len(coefs) - m):
                coef = coefs[m + j] * math.comb(m + j, j) * MID**j
                row = jnp.where((later == u) & (power == j), coef, row)
        rows_of.append(row)

    def late_tables(step, carry):
        send_rows(back, returned, 1, 8 + step * 7, 7)
        send_turn(turn_of, pieces_of, 2, bulk_after_three + step * bulk_four, bulk_four)
        at = pl.ds(pl.multiple_of(step * 32, 32), 32)
        rows = iota((128, BOX), 0)
        cells = lax.rem(rows, 8)
        values = cosines(length_z, iota((128, BOX), 1), slot_cells(length_z, cells))
        values = jnp.where((cells < 6) & (lax.div(rows, 8) == step), values, 0.0)
        edge_hi[step], edge_lo[step] = split(values)
        order = iota((32, BOX), 1)
        waves = lax.rem(order, PENCILS) * ROWS + lax.div(order, PENCILS)
        xt_hi[at, :], xt_lo[at, :] = split(cosines(length_x, waves, iota((32, BOX), 0) + step * 32))
        along_y = (iota((32, 128), 0) + step * 32).astype(F32) * (HALF_PI / BOX)
        along_y = along_y * along_y + MID
        for a in range(ROWS):
            wave = pencil * ROWS + a
            along_x = row_of(wave) * HALF_PI / row_of(length_x)
            t = along_y + (along_x * along_x)[:, :128]
            value = rows_of[7] * t + rows_of[6]
            for m in range(5, -1, -1):
                value = value * t + rows_of[m]
            lift[a, at, :] = jnp.where(jnp.full((1, 128), wave) < length_x, value, 0.0)
        return carry

    lax.fori_loop(0, 8, late_tables, 0)
    send_turn(turn_of, pieces_of, 2, bulk_after_four, PENCILS - bulk_after_four)
    rows = iota((64, BOX), 0)
    cells = lax.rem(rows, 8)
    values = jnp.where(cells < 6, cosines(length_z, iota((64, BOX), 1), slot_cells(length_z, cells)), 0.0)
    offset = along_z * (1.0 / MID) - 1.0
    raised, factor = jnp.ones_like(values), jnp.broadcast_to(offset, (64, BOX))
    for j in range(1, 8):
        raised = jnp.where(lax.div(rows, 8) >= j, raised * factor, raised)
    spread = dot3(split(values * raised), (tz_hi[...], tz_lo[...]))
    nothing = jnp.zeros_like(spread)
    for a in range(2):
        zt_hi[a], zt_lo[a] = split(jnp.concatenate([nothing, spread] if a else [spread, nothing], axis=0))

    wait_rows(back, returned, 1)
    come = split(returned[...])
    source, goal = iota((128, 128), 0), iota((128, 128), 1)
    half = iota((BOX, 128), 1) < 64
    planes = []
    for pair in range(2):
        lifted = []
        for a in (2 * pair, 2 * pair + 1):
            pick = (source == lax.div(goal, 64) * (8 * ROWS) + 8 * a + lax.rem(goal, 8)).astype(F32).astype(BF16)
            value = (dot(come[0], pick, 1, 0) + dot(come[1], pick, 1, 0)) * lift[a]
            lifted.append(value + pltpu.roll(value, 64, 1))
        plane = dot3((ty_hi[...], ty_lo[...]), split(jnp.where(half, lifted[0], lifted[1])))
        planes.append(plane.reshape(32, 8, 128))
    for parity, woven in enumerate(weave(*planes)):
        late_turn[:, parity] = woven
    own_late = pltpu.make_async_copy(late_turn_of(pencil), late_of(pencil), own_sem.at[3])
    own_late.start()

    def send_late(step, carry):
        send_turn(late_turn_of, late_of, 3, 1 + step * 9, 9)
        return carry

    lax.fori_loop(0, 7, send_late, 0)
    for a in range(ROWS):
        live = live_z * (jnp.full((1, BOX), pencil * ROWS + a) < length_x).astype(F32)
        for piece in range(2):
            at = slice(128 * piece, 128 * piece + 128)
            left = (come[0][at], come[1][at])
            gain = pushed[a, at, :]
            m1 = free[a, at, :] + gain * dot3(left, (edge_hi[a], edge_lo[a]))
            one_out[a, at, :] = m1
            two_out[a, at, :] = live * (twice[a, at, :] * m1 - m0[a, at, :]) + gain * dot3(
                left, (edge_hi[ROWS + a], edge_lo[ROWS + a])
            )
    own_turn.wait()
    own_late.wait()
    pltpu.make_async_remote_copy(
        src_ref=pieces.at[:, :, pl.ds(0, PENCILS - 1)],
        dst_ref=pieces.at[:, :, pl.ds(0, PENCILS - 1)],
        send_sem=send_sem.at[2],
        recv_sem=recv_sem.at[2],
        device_id=(dom, lax.rem(pencil + 1, PENCILS)),
        device_id_type=MESH,
    ).wait()
    pltpu.make_async_remote_copy(
        src_ref=late.at[pl.ds(0, PENCILS - 1)],
        dst_ref=late.at[pl.ds(0, PENCILS - 1)],
        send_sem=send_sem.at[3],
        recv_sem=recv_sem.at[3],
        device_id=(dom, lax.rem(pencil + 1, PENCILS)),
        device_id_type=MESH,
    ).wait()


def spread_kernel(pieces, late, xt_hi, xt_lo, zt_hi, zt_lo, one, two, one_out, two_out, pressure, sems):
    copies = [
        pltpu.make_async_copy(one, one_out, sems.at[0]),
        pltpu.make_async_copy(two, two_out, sems.at[1]),
    ]
    for copy in copies:
        copy.start()
    table = (xt_hi[...], xt_lo[...])
    for y in range(ROWS):
        rows = [late[pl.ds(ROWS * pair + y, PENCILS, stride=8), :] for pair in range(2)]
        rows = split(jnp.concatenate(rows, axis=0))
        extra = [dot3(rows, (zt_hi[a], zt_lo[a])) for a in range(2)]
        for side in range(2):
            parts = []
            for a in range(ROWS):
                pair, odd = a // 2, a % 2
                first = side * BOX * ROWS + pair * 8 * PENCILS + odd * ROWS + y
                piece = pieces[pl.ds(first, PENCILS, stride=8), :]
                parts.append(piece + extra[odd][PENCILS * pair : PENCILS * (pair + 1), 128 * side : 128 * side + 128])
            pressure[:, y, 128 * side : 128 * side + 128] = dot3(table, split(jnp.concatenate(parts, axis=0)))
    for copy in copies:
        copy.wait()


def on_device(modes_now, modes_prev, extents, strips):
    vmem, hbm, anywhere = (
        pl.BlockSpec(memory_space=space) for space in (pltpu.VMEM, pltpu.HBM, pl.ANY)
    )
    field = jax.ShapeDtypeStruct((ROWS, BOX, BOX), F32)
    half_table = jax.ShapeDtypeStruct((BOX, BOX), BF16)
    wide_table = jax.ShapeDtypeStruct((2, 128, BOX), BF16)
    one, two, pieces, late, xt_hi, xt_lo, zt_hi, zt_lo = pl.pallas_call(
        coupled_kernel,
        out_shape=(
            field,
            field,
            jax.ShapeDtypeStruct((2, 2, PENCILS, 8, 128), F32),
            jax.ShapeDtypeStruct((PENCILS, 8, 128), F32),
            half_table,
            half_table,
            wide_table,
            wide_table,
        ),
        in_specs=[hbm] * 4,
        out_specs=[vmem] * 8,
        scratch_shapes=[pltpu.VMEM((ROWS, BOX, BOX), F32)] * 5
        + [pltpu.VMEM((EVERYONE, 128), F32)] * 4
        + [pltpu.VMEM((DOMS, BOX, BOX), BF16)] * 2
        + [pltpu.VMEM((DOMS, 2, 64, 128), F32)]
        + [pltpu.VMEM((2 * ROWS, 128, BOX), BF16)] * 2
        + [pltpu.VMEM((BOX, BOX), BF16)] * 4
        + [pltpu.VMEM((ROWS, BOX, BOX), BF16)] * 2
        + [pltpu.VMEM((2, 2, PENCILS // 2, 2, 8, 128), F32)]
        + [pltpu.VMEM((ROWS, BOX, 128), F32), pltpu.VMEM((PENCILS // 2, 2, 8, 128), F32)]
        + [pltpu.SMEM((2, DOMS), I32), pltpu.SMEM((STRIPS, 6), I32)]
        + [pltpu.SemaphoreType.DMA((4,))] * 4,
        compiler_params=pltpu.CompilerParams(has_side_effects=True, collective_id=1, vmem_limit_bytes=199 << 18),
        name="coupled",
    )(extents.T, strips, modes_now[0], modes_prev[0])
    one, two, pressure = pl.pallas_call(
        spread_kernel,
        out_shape=(field, field, jax.ShapeDtypeStruct((BOX, ROWS, BOX), F32)),
        in_specs=[vmem] * 8,
        out_specs=[anywhere, anywhere, vmem],
        scratch_shapes=[pltpu.SemaphoreType.DMA((2,))],
        compiler_params=pltpu.CompilerParams(vmem_limit_bytes=24 << 20),
        name="spread",
    )(pieces.reshape(2 * BOX * ROWS, 128), late.reshape(PENCILS * 8, 128), xt_hi, xt_lo, zt_hi, zt_lo, one, two)
    return (two[None], one[None], pressure[None])


def solution(mesh):
    return jax.shard_map(
        on_device,
        mesh=mesh,
        in_specs=(P("dom", "pencil", None, None), P("dom", "pencil", None, None), P(), P()),
        out_specs=(
            P("dom", "pencil", None, None),
            P("dom", "pencil", None, None),
            P("dom", None, "pencil", None),
        ),
        check_vma=False,
    )
```

```python
import functools
import math

import jax
import jax.numpy as jnp
from jax import lax
from jax.experimental import pallas as pl
from jax.experimental.pallas import tpu as pltpu
from jax.sharding import PartitionSpec as P

MESH = pl.DeviceIdType.MESH
F32, BF16, I32 = jnp.float32, jnp.bfloat16, jnp.int32
DOMS, PENCILS, BOX, ROWS = 4, 64, 256, 4
EVERYONE = DOMS * PENCILS
STRIPS = 8
HALF_PI = math.pi / 2.0
COUPLING = (1.5, -0.15, 2.0 / 180.0)
GAIN = (
    0.9999999999869928, -0.08333333316111119, 0.0027777774047159443, -4.960287119518586e-05,
    5.510286659542367e-07, -4.151822786228911e-09, 2.058914415718572e-11,
)
PUSHED_GAIN = (
    1.9999999838483329, -1.1666663858596251, 0.17222142001421806, -0.012598331258825314,
    0.0005628010719150018, -1.6955597515164814e-05, 3.5301674212625207e-07, -4.241805096348839e-09,
)
MID = math.pi**2 / 8.0
PARTS = 2
BULK = (1,2,12,0)
SINE = (
    1.5707963267681446, -0.6459640955780578, 0.07969260371703452, -0.004681657795344663,
    0.00016025469086571314, -3.431829236433259e-06,
)


def poly(coefs, t):
    value = jnp.full_like(t, coefs[-1])
    for coef in coefs[-2::-1]:
        value = value * t + coef
    return value


def split(value):
    high = value.astype(BF16)
    return high, (value - high.astype(F32)).astype(BF16)


def dot(left, right, left_dim, right_dim):
    return lax.dot_general(left, right, (((left_dim,), (right_dim,)), ((), ())), preferred_element_type=F32)


def dot3(left, right, left_dim=1, right_dim=0):
    return (
        dot(left[0], right[0], left_dim, right_dim)
        + dot(left[0], right[1], left_dim, right_dim)
        + dot(left[1], right[0], left_dim, right_dim)
    )


def dot_thin(value, right, right_dim):
    rows = value.shape[0]
    high = value.astype(BF16).astype(F32)
    left = jnp.concatenate([high, value - high], axis=0).astype(BF16)
    total = dot(left, right[0], 1, right_dim) + dot(left, right[1], 1, right_dim)
    return total[:rows] + total[rows:]


def iota(shape, dim):
    return lax.broadcasted_iota(I32, shape, dim)


def row_of(scalar):
    return jnp.full((1, BOX), scalar.astype(F32))


def cosines(length, waves, cells):
    width = max(waves.shape[1], cells.shape[1])
    long = jnp.full((1, width), length.astype(F32))
    inverse = 1.0 / long
    n = (waves * (2 * cells + 1)).astype(F32)
    turns = jnp.floor(n * (0.25 * inverse) + 0.5)
    u = 1.0 - jnp.abs(n - turns * (4.0 * long)) * inverse
    scale = jnp.where(waves == 0, jnp.sqrt(inverse), jnp.sqrt(2.0 * inverse))
    value = scale * u * poly(SINE, u * u)
    return jnp.where((waves < length) & (cells < length), value, 0.0)


def slot_cells(length_z, slots):
    return jnp.where(slots < 3, slots, length_z - 1 - (slots - 3))


def coupled_kernel(
    ext_in, strips_in, now, prev,
    one_out, two_out, pieces, late, xt_hi, xt_lo, zt_hi, zt_lo,
    m0, m_old, pushed, twice, free, sent, got, back, returned,
    tx_hi, tx_lo, response, edge_hi, edge_lo, tz_hi, tz_lo, ty_hi, ty_lo, mid_hi, mid_lo, turn, lift, late_turn, ext, strips,
    load_sem, own_sem, send_sem, recv_sem,
):
    dom, pencil = lax.axis_index("dom"), lax.axis_index("pencil")
    me = dom * PENCILS + pencil
    load_now = pltpu.make_async_copy(now, m0, load_sem.at[0])
    load_prev = pltpu.make_async_copy(prev, m_old, load_sem.at[1])
    small_loads = [
        pltpu.make_async_copy(ext_in, ext, load_sem.at[2]),
        pltpu.make_async_copy(strips_in, strips, load_sem.at[3]),
    ]
    for load in (*small_loads, load_now, load_prev):
        load.start()
    barrier = pltpu.get_barrier_semaphore()

    doms = [lax.rem(dom + d, DOMS) for d in range(DOMS)]

    def devices(shift, own_pencil=False):
        around = pencil if own_pencil else lax.rem(pencil + shift, PENCILS)
        return [(d * PENCILS + around, (d, around)) for d in (doms[1:] if own_pencil else doms)]

    def greet(first, count):
        for shift in range(count):
            for _, device in devices(first + shift):
                pl.semaphore_signal(barrier, inc=1, device_id=device, device_id_type=MESH)

    def greet_own():
        for _, device in devices(0, True):
            pl.semaphore_signal(barrier, inc=1, device_id=device, device_id_type=MESH)

    def send_row(source, target, leg, peer, device):
        pltpu.make_async_remote_copy(
            src_ref=source.at[pl.ds(peer, 1)],
            dst_ref=target.at[pl.ds(me, 1)],
            send_sem=send_sem.at[leg],
            recv_sem=recv_sem.at[leg],
            device_id=device,
            device_id_type=MESH,
        ).start()

    def send_rows(source, target, leg, first, count):
        for shift in range(count):
            for peer, device in devices(first + shift):
                send_row(source, target, leg, peer, device)

    def send_own(source, target, leg):
        for peer, device in devices(0, True):
            send_row(source, target, leg, peer, device)

    def send_turn(source, target, leg, first, count):
        for j in range(count):
            peer = lax.rem(pencil + first + j, PENCILS)
            pltpu.make_async_remote_copy(
                src_ref=source(peer),
                dst_ref=target(pencil),
                send_sem=send_sem.at[leg],
                recv_sem=recv_sem.at[leg],
                device_id=(dom, peer),
                device_id_type=MESH,
            ).start()

    def turn_of(peer):
        return turn.at[:, :, lax.div(peer, 2), lax.rem(peer, 2)]

    def pieces_of(peer):
        return pieces.at[:, :, peer]

    def late_turn_of(peer):
        return late_turn.at[lax.div(peer, 2), lax.rem(peer, 2)]

    def late_of(peer):
        return late.at[peer]

    def wait_rows(source, target, leg):
        pltpu.make_async_copy(source.at[pl.ds(me, 1)], target.at[pl.ds(me, 1)], own_sem.at[leg]).wait()
        pltpu.make_async_remote_copy(
            src_ref=source.at[pl.ds(0, EVERYONE - 1)],
            dst_ref=target.at[pl.ds(0, EVERYONE - 1)],
            send_sem=send_sem.at[leg],
            recv_sem=recv_sem.at[leg],
            device_id=(doms[1], pencil),
            device_id_type=MESH,
        ).wait()

    greet_own()
    greet(1, 7)
    for load in small_loads:
        load.wait()
    length_x, length_z = ext[0, dom], ext[1, dom]

    lanes = iota((BOX, 128), 1)
    slots = lax.rem(lanes, 8)
    table = cosines(length_z, iota((BOX, 128), 0), slot_cells(length_z, slots))
    face_hi, face_lo = split(jnp.where(slots < 6, table, 0.0))
    waves_z = iota((1, BOX), 1)
    along_z = waves_z.astype(F32) * HALF_PI / row_of(length_z)
    along_z = along_z * along_z
    live_z = (waves_z < length_z).astype(F32)
    def first_tables(step, carry):
        at = pl.ds(pl.multiple_of(step * 32, 32), 32)
        near, far = iota((32, BOX), 0) + step * 32, iota((32, BOX), 1)
        tz_hi[at, :], tz_lo[at, :] = split(cosines(length_z, near, far))
        ty_hi[at, :], ty_lo[at, :] = split(cosines(jnp.int32(BOX), far, near))
        greet(8 + step * 3, 3)
        return carry

    lax.fori_loop(0, 8, first_tables, 0)
    load_now.wait()
    load_prev.wait()
    block = 32
    groups = lax.div(iota((block, 128), 1), 8)

    def gather_faces(step, carry):
        at = pl.ds(pl.multiple_of(step * block, block), block)
        along_y = (iota((block, BOX), 0) + step * block).astype(F32) * (HALF_PI / BOX)
        along_y = along_y * along_y
        message = jnp.zeros((block, 128), F32)
        for a in range(ROWS):
            wave = pencil * ROWS + a
            along_x = row_of(wave) * HALF_PI / row_of(length_x)
            live = live_z * (jnp.full((1, BOX), wave) < length_x).astype(F32)
            t = along_y + (along_z + along_x * along_x)
            gain = poly(GAIN, t)
            twice_cos = 2.0 - t * gain
            here = m0[a, at, :]
            ahead = live * (twice_cos * here - m_old[a, at, :])
            pushed[a, at, :] = live * gain
            twice[a, at, :] = twice_cos
            free[a, at, :] = ahead
            base = live * (twice_cos * ahead - here)
            mid_hi[a, at, :], mid_lo[a, at, :] = split(dot3(split(base), (tz_hi[...], tz_lo[...])))
            for u, value in enumerate((here, ahead)):
                faces = dot3(split(value), (face_hi, face_lo))
                message = jnp.where(groups == u * ROWS + a, faces, message)
        sent[at, :] = message
        greet(32 + step * 4, 4)
        return carry

    lax.fori_loop(0, BOX // block, gather_faces, 0)
    top = iota((32, 8, BOX), 1) < 4

    def weave(first, second):
        upper = top[:, :, : first.shape[2]]
        even = jnp.where(upper, first, pltpu.roll(second, 4, 1))
        return even, jnp.where(upper, pltpu.roll(first, 4, 1), second)

    for pair in range(2):
        planes = [
            dot3((ty_hi[...], ty_lo[...]), (mid_hi[a], mid_lo[a])).reshape(32, 8, BOX)
            for a in (2 * pair, 2 * pair + 1)
        ]
        for parity, woven in enumerate(weave(*planes)):
            for side in range(2):
                turn[side, pair, :, parity] = woven[:, :, 128 * side : 128 * side + 128]
    pl.semaphore_wait(barrier, EVERYONE - 1)
    pltpu.make_async_copy(sent.at[pl.ds(me, 1)], got.at[pl.ds(me, 1)], own_sem.at[0]).start()
    send_own(sent, got, 0)
    send_rows(sent, got, 0, 1, 7)
    own_turn = pltpu.make_async_copy(turn_of(pencil), pieces_of(pencil), own_sem.at[2])
    own_turn.start()
    bulk_one, bulk_two, bulk_three, bulk_four = BULK
    bulk_after_one = 1 + DOMS * ROWS * bulk_one
    bulk_after_two = bulk_after_one + DOMS * 2 * bulk_two
    bulk_after_three = bulk_after_two + bulk_three
    bulk_after_four = bulk_after_three + 8 * bulk_four

    def x_tables(step, carry):
        send_rows(sent, got, 0, 8 + step * 3, 3)
        send_turn(turn_of, pieces_of, 2, 1 + step * bulk_one, bulk_one)
        part, a = lax.div(step, ROWS), lax.rem(step, ROWS)
        at = pl.ds(pl.multiple_of(a * PENCILS, PENCILS), PENCILS)
        high, low = split(
            cosines(ext[0, part], iota((PENCILS, BOX), 0) * ROWS + a, iota((PENCILS, BOX), 1))
        )
        tx_hi[part, at, :] = high
        tx_lo[part, at, :] = low
        return carry

    lax.fori_loop(0, DOMS * ROWS, x_tables, 0)

    def responses(step, carry):
        send_rows(sent, got, 0, 56 + step, 1)
        send_turn(turn_of, pieces_of, 2, bulk_after_one + step * bulk_two, bulk_two)
        part, half = lax.div(step, 2), lax.rem(step, 2)
        long_x, long_z = ext[0, part], ext[1, part]
        slot = iota((8, BOX), 0)
        rows = jnp.where(slot < 6, cosines(long_z, iota((8, BOX), 1), slot_cells(long_z, slot)), 0.0)
        pairs = jnp.concatenate([rows * rows[i : i + 1] for i in range(8)], axis=0)
        order = iota((128, BOX), 0) + half * 128
        waves = lax.rem(order, PENCILS) * ROWS + lax.div(order, PENCILS)
        along_x = waves.astype(F32) * HALF_PI / row_of(long_x)
        across = waves_z.astype(F32) * HALF_PI / row_of(long_z)
        along_y = row_of(me) * (HALF_PI / BOX)
        gain = poly(GAIN, along_x * along_x + (across * across + along_y * along_y))
        gain = jnp.where((waves < long_x) & (iota((128, BOX), 1) < long_z), gain, 0.0)
        response[part, half] = dot3(split(pairs), split(gain), 1, 1)
        return carry

    lax.fori_loop(0, DOMS * 2, responses, 0)

    def of_strip(strip_index, field):
        value = jnp.zeros_like(strip_index)
        for e in range(STRIPS):
            value = jnp.where(strip_index == e, strips[e, field], value)
        return value

    wide = iota((8 * STRIPS, 32), 0)
    index, depth = lax.div(wide, 8), lax.rem(wide, 8)
    column = iota((8 * STRIPS, 32), 1)
    part, slot = lax.div(column, 8), lax.rem(column, 8)
    face = of_strip(index, 2)

    def weights(parts, side):
        other = slot - 3 * side
        reach = depth + other
        value = jnp.where(reach == 0, 0.25 * COUPLING[0], jnp.where(reach == 1, 0.25 * COUPLING[1], 0.25 * COUPLING[2]))
        hit = (parts == part) & (other >= 0) & (other < 3) & (depth < 3) & (reach < 3)
        return jnp.where(hit, value, 0.0)

    takes = split(jnp.concatenate([weights(of_strip(index, 1), 1 - face), weights(of_strip(index, 0), face)], axis=0))
    tall = iota((32, 8 * STRIPS), 1)
    index, depth = lax.div(tall, 8), lax.rem(tall, 8)
    column = iota((32, 8 * STRIPS), 0)
    part, slot = lax.div(column, 8), lax.rem(column, 8)
    gives = (part == of_strip(index, 0)) & (slot == 3 * of_strip(index, 2) + depth) & (depth < 3)
    gives = jnp.where(gives, 1.0, 0.0).astype(BF16)
    index = lax.div(iota((8 * STRIPS, BOX), 0), 8)
    cells = iota((8 * STRIPS, BOX), 1)
    start = of_strip(index, 3)
    inside = (cells >= start) & (cells < start + of_strip(index, 5))

    def force(face_modes):
        faces = jnp.concatenate(
            [dot_thin(face_modes[p], (tx_hi[p], tx_lo[p]), 0) for p in range(DOMS)], axis=0
        )
        taken = dot3(takes, split(faces))
        shifted = [
            pltpu.roll(taken[8 * e : 8 * e + 8], lax.rem(strips[e, 3] - strips[e, 4] + BOX, BOX), 1)
            for e in range(STRIPS)
        ]
        gap = split(jnp.where(inside, jnp.concatenate(shifted, axis=0) - taken[8 * STRIPS :], 0.0))
        forcing = dot(gives, gap[0], 1, 0) + dot(gives, gap[1], 1, 0)
        return [dot_thin(forcing[8 * p : 8 * p + 8], (tx_hi[p], tx_lo[p]), 1) for p in range(DOMS)]

    wait_rows(sent, got, 0)
    send_turn(turn_of, pieces_of, 2, bulk_after_two, bulk_three)
    first, second = [], []
    for pair in range(2):
        turned = got[128 * pair : 128 * pair + 128, :].T
        for p in range(2):
            for u, held in enumerate((first, second)):
                held.append(
                    jnp.concatenate(
                        [
                            turned[8 * (u * ROWS + a) : 8 * (u * ROWS + a) + 8, PENCILS * p : PENCILS * (p + 1)]
                            for a in range(ROWS)
                        ],
                        axis=1,
                    )
                )
    force_one = force(first)
    answered = []
    for p in range(DOMS):
        both = jnp.concatenate([response[p, 0], response[p, 1]], axis=1).reshape(8, 8, BOX)
        answered.append(second[p] + jnp.sum(both * force_one[p][None], axis=1))
    force_two = force(answered)
    for pair in range(2):
        rows = [
            jnp.concatenate(
                [forces[2 * pair + p][:, PENCILS * a : PENCILS * (a + 1)] for p in range(2)], axis=1
            )
            for forces in (force_one, force_two)
            for a in range(ROWS)
        ]
        rows.append(jnp.zeros((64, 128), F32))
        back[128 * pair : 128 * pair + 128, :] = jnp.concatenate(rows, axis=0).T
    pltpu.make_async_copy(back.at[pl.ds(me, 1)], returned.at[pl.ds(me, 1)], own_sem.at[1]).start()
    send_own(back, returned, 1)
    send_rows(back, returned, 1, 1, 7)

    chunk = iota((1, 128), 1)
    later, power = lax.div(chunk, 64), lax.rem(lax.div(chunk, 8), 8)
    rows_of = []
    for m in range(8):
        row = jnp.zeros((1, 128), F32)
        for u, coefs in enumerate((PUSHED_GAIN, GAIN)):
            for j in range(len(coefs) - m):
                coef = coefs[m + j] * math.comb(m + j, j) * MID**j
                row = jnp.where((later == u) & (power == j), coef, row)
        rows_of.append(row)

    def late_tables(step, carry):
        send_rows(back, returned, 1, 8 + step * 7, 7)
        send_turn(turn_of, pieces_of, 2, bulk_after_three + step * bulk_four, bulk_four)
        at = pl.ds(pl.multiple_of(step * 32, 32), 32)
        rows = iota((128, BOX), 0)
        cells = lax.rem(rows, 8)
        values = cosines(length_z, iota((128, BOX), 1), slot_cells(length_z, cells))
        values = jnp.where((cells < 6) & (lax.div(rows, 8) == step), values, 0.0)
        edge_hi[step], edge_lo[step] = split(values)
        order = iota((32, BOX), 1)
        waves = lax.rem(order, PENCILS) * ROWS + lax.div(order, PENCILS)
        xt_hi[at, :], xt_lo[at, :] = split(cosines(length_x, waves, iota((32, BOX), 0) + step * 32))
        along_y = (iota((32, 128), 0) + step * 32).astype(F32) * (HALF_PI / BOX)
        along_y = along_y * along_y + MID
        for a in range(ROWS):
            wave = pencil * ROWS + a
            along_x = row_of(wave) * HALF_PI / row_of(length_x)
            t = along_y + (along_x * along_x)[:, :128]
            value = rows_of[7] * t + rows_of[6]
            for m in range(5, -1, -1):
                value = value * t + rows_of[m]
            lift[a, at, :] = jnp.where(jnp.full((1, 128), wave) < length_x, value, 0.0)
        return carry

    lax.fori_loop(0, 8, late_tables, 0)
    send_turn(turn_of, pieces_of, 2, bulk_after_four, PENCILS - bulk_after_four)
    rows = iota((64, BOX), 0)
    cells = lax.rem(rows, 8)
    values = jnp.where(cells < 6, cosines(length_z, iota((64, BOX), 1), slot_cells(length_z, cells)), 0.0)
    offset = along_z * (1.0 / MID) - 1.0
    raised, factor = jnp.ones_like(values), jnp.broadcast_to(offset, (64, BOX))
    for j in range(1, 8):
        raised = jnp.where(lax.div(rows, 8) >= j, raised * factor, raised)
    spread = dot3(split(values * raised), (tz_hi[...], tz_lo[...]))
    nothing = jnp.zeros_like(spread)
    for a in range(2):
        zt_hi[a], zt_lo[a] = split(jnp.concatenate([nothing, spread] if a else [spread, nothing], axis=0))

    wait_rows(back, returned, 1)
    come = split(returned[...])
    source, goal = iota((128, 128), 0), iota((128, 128), 1)
    half = iota((BOX, 128), 1) < 64
    planes = []
    for pair in range(2):
        lifted = []
        for a in (2 * pair, 2 * pair + 1):
            pick = (source == lax.div(goal, 64) * (8 * ROWS) + 8 * a + lax.rem(goal, 8)).astype(F32).astype(BF16)
            value = (dot(come[0], pick, 1, 0) + dot(come[1], pick, 1, 0)) * lift[a]
            lifted.append(value + pltpu.roll(value, 64, 1))
        plane = dot3((ty_hi[...], ty_lo[...]), split(jnp.where(half, lifted[0], lifted[1])))
        planes.append(plane.reshape(32, 8, 128))
    for parity, woven in enumerate(weave(*planes)):
        late_turn[:, parity] = woven
    own_late = pltpu.make_async_copy(late_turn_of(pencil), late_of(pencil), own_sem.at[3])
    own_late.start()

    def send_late(step, carry):
        send_turn(late_turn_of, late_of, 3, 1 + step * 9, 9)
        return carry

    lax.fori_loop(0, 7, send_late, 0)
    for a in range(ROWS):
        live = live_z * (jnp.full((1, BOX), pencil * ROWS + a) < length_x).astype(F32)
        for piece in range(2):
            at = slice(128 * piece, 128 * piece + 128)
            left = (come[0][at], come[1][at])
            gain = pushed[a, at, :]
            m1 = free[a, at, :] + gain * dot3(left, (edge_hi[a], edge_lo[a]))
            one_out[a, at, :] = m1
            two_out[a, at, :] = live * (twice[a, at, :] * m1 - m0[a, at, :]) + gain * dot3(
                left, (edge_hi[ROWS + a], edge_lo[ROWS + a])
            )
    own_turn.wait()
    own_late.wait()
    pltpu.make_async_remote_copy(
        src_ref=pieces.at[:, :, pl.ds(0, PENCILS - 1)],
        dst_ref=pieces.at[:, :, pl.ds(0, PENCILS - 1)],
        send_sem=send_sem.at[2],
        recv_sem=recv_sem.at[2],
        device_id=(dom, lax.rem(pencil + 1, PENCILS)),
        device_id_type=MESH,
    ).wait()
    pltpu.make_async_remote_copy(
        src_ref=late.at[pl.ds(0, PENCILS - 1)],
        dst_ref=late.at[pl.ds(0, PENCILS - 1)],
        send_sem=send_sem.at[3],
        recv_sem=recv_sem.at[3],
        device_id=(dom, lax.rem(pencil + 1, PENCILS)),
        device_id_type=MESH,
    ).wait()


def spread_kernel(pieces, late, xt_hi, xt_lo, zt_hi, zt_lo, one, two, one_out, two_out, pressure, held, sems):
    copies = [
        pltpu.make_async_copy(one, one_out, sems.at[0]),
        pltpu.make_async_copy(two, two_out, sems.at[1]),
    ]
    for copy in copies:
        copy.start()
    fields = []
    for y in range(ROWS):
        rows = [late[pl.ds(ROWS * pair + y, PENCILS, stride=8), :] for pair in range(2)]
        rows = split(jnp.concatenate(rows, axis=0))
        extra = [dot3(rows, (zt_hi[a], zt_lo[a])) for a in range(2)]
        parts = []
        for a in range(ROWS):
            pair, odd = a // 2, a % 2
            sides = [
                pieces[pl.ds(side * BOX * ROWS + pair * 8 * PENCILS + odd * ROWS + y, PENCILS, stride=8), :]
                for side in range(2)
            ]
            parts.append(jnp.concatenate(sides, axis=1) + extra[odd][PENCILS * pair : PENCILS * (pair + 1)])
        fields.append(split(jnp.concatenate(parts, axis=0)))
    for part in range(PARTS):
        at = slice(part * (BOX // PARTS), (part + 1) * (BOX // PARTS))
        table = (xt_hi[at, :], xt_lo[at, :])
        for y in range(ROWS):
            held[at, y, :] = dot3(table, fields[y])
        copy = pltpu.make_async_copy(held.at[at], pressure.at[at], sems.at[2 + part])
        copy.start()
        copies.append(copy)
    for copy in copies:
        copy.wait()


def on_device(modes_now, modes_prev, extents, strips):
    vmem, hbm, anywhere = (
        pl.BlockSpec(memory_space=space) for space in (pltpu.VMEM, pltpu.HBM, pl.ANY)
    )
    field = jax.ShapeDtypeStruct((ROWS, BOX, BOX), F32)
    half_table = jax.ShapeDtypeStruct((BOX, BOX), BF16)
    wide_table = jax.ShapeDtypeStruct((2, 128, BOX), BF16)
    one, two, pieces, late, xt_hi, xt_lo, zt_hi, zt_lo = pl.pallas_call(
        coupled_kernel,
        out_shape=(
            field,
            field,
            jax.ShapeDtypeStruct((2, 2, PENCILS, 8, 128), F32),
            jax.ShapeDtypeStruct((PENCILS, 8, 128), F32),
            half_table,
            half_table,
            wide_table,
            wide_table,
        ),
        in_specs=[hbm] * 4,
        out_specs=[vmem] * 8,
        scratch_shapes=[pltpu.VMEM((ROWS, BOX, BOX), F32)] * 5
        + [pltpu.VMEM((EVERYONE, 128), F32)] * 4
        + [pltpu.VMEM((DOMS, BOX, BOX), BF16)] * 2
        + [pltpu.VMEM((DOMS, 2, 64, 128), F32)]
        + [pltpu.VMEM((2 * ROWS, 128, BOX), BF16)] * 2
        + [pltpu.VMEM((BOX, BOX), BF16)] * 4
        + [pltpu.VMEM((ROWS, BOX, BOX), BF16)] * 2
        + [pltpu.VMEM((2, 2, PENCILS // 2, 2, 8, 128), F32)]
        + [pltpu.VMEM((ROWS, BOX, 128), F32), pltpu.VMEM((PENCILS // 2, 2, 8, 128), F32)]
        + [pltpu.SMEM((2, DOMS), I32), pltpu.SMEM((STRIPS, 6), I32)]
        + [pltpu.SemaphoreType.DMA((4,))] * 4,
        compiler_params=pltpu.CompilerParams(has_side_effects=True, collective_id=1, vmem_limit_bytes=199 << 18),
        name="coupled",
    )(extents.T, strips, modes_now[0], modes_prev[0])
    one, two, pressure = pl.pallas_call(
        spread_kernel,
        out_shape=(field, field, jax.ShapeDtypeStruct((BOX, ROWS, BOX), F32)),
        in_specs=[vmem] * 8,
        out_specs=[anywhere] * 3,
        scratch_shapes=[pltpu.VMEM((BOX, ROWS, BOX), F32), pltpu.SemaphoreType.DMA((2 + PARTS,))],
        compiler_params=pltpu.CompilerParams(vmem_limit_bytes=24 << 20),
        name="spread",
    )(pieces.reshape(2 * BOX * ROWS, 128), late.reshape(PENCILS * 8, 128), xt_hi, xt_lo, zt_hi, zt_lo, one, two)
    return (two[None], one[None], pressure[None])


def solution(mesh):
    return jax.shard_map(
        on_device,
        mesh=mesh,
        in_specs=(P("dom", "pencil", None, None), P("dom", "pencil", None, None), P(), P()),
        out_specs=(
            P("dom", "pencil", None, None),
            P("dom", "pencil", None, None),
            P("dom", None, "pencil", None),
        ),
        check_vma=False,
    )
```

```python
import functools
import math

import jax
import jax.numpy as jnp
from jax import lax
from jax.experimental import pallas as pl
from jax.experimental.pallas import tpu as pltpu
from jax.sharding import PartitionSpec as P

MESH = pl.DeviceIdType.MESH
F32, BF16, I32 = jnp.float32, jnp.bfloat16, jnp.int32
DOMS, PENCILS, BOX, ROWS = 4, 64, 256, 4
EVERYONE = DOMS * PENCILS
STRIPS = 8
HALF_PI = math.pi / 2.0
COUPLING = (1.5, -0.15, 2.0 / 180.0)
GAIN = (
    0.9999999999869928, -0.08333333316111119, 0.0027777774047159443, -4.960287119518586e-05,
    5.510286659542367e-07, -4.151822786228911e-09, 2.058914415718572e-11,
)
PUSHED_GAIN = (
    1.9999999838483329, -1.1666663858596251, 0.17222142001421806, -0.012598331258825314,
    0.0005628010719150018, -1.6955597515164814e-05, 3.5301674212625207e-07, -4.241805096348839e-09,
)
MID = math.pi**2 / 8.0
PARTS = 2
BULK = (1,2,12,0)
SINE = (
    1.5707963267681446, -0.6459640955780578, 0.07969260371703452, -0.004681657795344663,
    0.00016025469086571314, -3.431829236433259e-06,
)


def poly(coefs, t):
    value = jnp.full_like(t, coefs[-1])
    for coef in coefs[-2::-1]:
        value = value * t + coef
    return value


def split(value):
    high = value.astype(BF16)
    return high, (value - high.astype(F32)).astype(BF16)


def dot(left, right, left_dim, right_dim):
    return lax.dot_general(left, right, (((left_dim,), (right_dim,)), ((), ())), preferred_element_type=F32)


def dot3(left, right, left_dim=1, right_dim=0):
    return (
        dot(left[0], right[0], left_dim, right_dim)
        + dot(left[0], right[1], left_dim, right_dim)
        + dot(left[1], right[0], left_dim, right_dim)
    )


def dot_thin(value, right, right_dim):
    rows = value.shape[0]
    high = value.astype(BF16).astype(F32)
    left = jnp.concatenate([high, value - high], axis=0).astype(BF16)
    total = dot(left, right[0], 1, right_dim) + dot(left, right[1], 1, right_dim)
    return total[:rows] + total[rows:]


def iota(shape, dim):
    return lax.broadcasted_iota(I32, shape, dim)


def row_of(scalar):
    return jnp.full((1, BOX), scalar.astype(F32))


def cosines(length, waves, cells):
    width = max(waves.shape[1], cells.shape[1])
    long = jnp.full((1, width), length.astype(F32))
    inverse = 1.0 / long
    n = (waves * (2 * cells + 1)).astype(F32)
    turns = jnp.floor(n * (0.25 * inverse) + 0.5)
    u = 1.0 - jnp.abs(n - turns * (4.0 * long)) * inverse
    scale = jnp.where(waves == 0, jnp.sqrt(inverse), jnp.sqrt(2.0 * inverse))
    value = scale * u * poly(SINE, u * u)
    return jnp.where((waves < length) & (cells < length), value, 0.0)


def slot_cells(length_z, slots):
    return jnp.where(slots < 3, slots, length_z - 1 - (slots - 3))


def coupled_kernel(
    ext_in, strips_in, now, prev,
    one_out, two_out, pieces, late, xt_hi, xt_lo, zt_hi, zt_lo,
    m0, m_old, pushed, twice, free, sent, got, back, returned,
    tx_hi, tx_lo, response, edge_hi, edge_lo, tz_hi, tz_lo, ty_hi, ty_lo, mid_hi, mid_lo, turn, lift, late_turn, ext, strips,
    load_sem, own_sem, send_sem, recv_sem,
):
    dom, pencil = lax.axis_index("dom"), lax.axis_index("pencil")
    me = dom * PENCILS + pencil
    load_now = pltpu.make_async_copy(now, m0, load_sem.at[0])
    load_prev = pltpu.make_async_copy(prev, m_old, load_sem.at[1])
    small_loads = [
        pltpu.make_async_copy(ext_in, ext, load_sem.at[2]),
        pltpu.make_async_copy(strips_in, strips, load_sem.at[3]),
    ]
    for load in (*small_loads, load_now, load_prev):
        load.start()
    barrier = pltpu.get_barrier_semaphore()

    doms = [lax.rem(dom + d, DOMS) for d in range(DOMS)]

    def devices(shift, own_pencil=False):
        around = pencil if own_pencil else lax.rem(pencil + shift, PENCILS)
        return [(d * PENCILS + around, (d, around)) for d in (doms[1:] if own_pencil else doms)]

    def greet(first, count):
        for shift in range(count):
            for _, device in devices(first + shift):
                pl.semaphore_signal(barrier, inc=1, device_id=device, device_id_type=MESH)

    def greet_own():
        for _, device in devices(0, True):
            pl.semaphore_signal(barrier, inc=1, device_id=device, device_id_type=MESH)

    def send_row(source, target, leg, peer, device):
        pltpu.make_async_remote_copy(
            src_ref=source.at[pl.ds(peer, 1)],
            dst_ref=target.at[pl.ds(me, 1)],
            send_sem=send_sem.at[leg],
            recv_sem=recv_sem.at[leg],
            device_id=device,
            device_id_type=MESH,
        ).start()

    def send_rows(source, target, leg, first, count):
        for shift in range(count):
            for peer, device in devices(first + shift):
                send_row(source, target, leg, peer, device)

    def send_own(source, target, leg):
        for peer, device in devices(0, True):
            send_row(source, target, leg, peer, device)

    def send_turn(source, target, leg, first, count):
        for j in range(count):
            peer = lax.rem(pencil + first + j, PENCILS)
            pltpu.make_async_remote_copy(
                src_ref=source(peer),
                dst_ref=target(pencil),
                send_sem=send_sem.at[leg],
                recv_sem=recv_sem.at[leg],
                device_id=(dom, peer),
                device_id_type=MESH,
            ).start()

    def turn_of(peer):
        return turn.at[:, :, lax.div(peer, 2), lax.rem(peer, 2)]

    def pieces_of(peer):
        return pieces.at[:, :, peer]

    def late_turn_of(peer):
        return late_turn.at[lax.div(peer, 2), lax.rem(peer, 2)]

    def late_of(peer):
        return late.at[peer]

    def wait_rows(source, target, leg):
        pltpu.make_async_copy(source.at[pl.ds(me, 1)], target.at[pl.ds(me, 1)], own_sem.at[leg]).wait()
        pltpu.make_async_remote_copy(
            src_ref=source.at[pl.ds(0, EVERYONE - 1)],
            dst_ref=target.at[pl.ds(0, EVERYONE - 1)],
            send_sem=send_sem.at[leg],
            recv_sem=recv_sem.at[leg],
            device_id=(doms[1], pencil),
            device_id_type=MESH,
        ).wait()

    greet_own()
    greet(1, 7)
    for load in small_loads:
        load.wait()
    length_x, length_z = ext[0, dom], ext[1, dom]

    lanes = iota((BOX, 128), 1)
    slots = lax.rem(lanes, 8)
    table = cosines(length_z, iota((BOX, 128), 0), slot_cells(length_z, slots))
    face_hi, face_lo = split(jnp.where(slots < 6, table, 0.0))
    waves_z = iota((1, BOX), 1)
    along_z = waves_z.astype(F32) * HALF_PI / row_of(length_z)
    along_z = along_z * along_z
    live_z = (waves_z < length_z).astype(F32)
    def first_tables(step, carry):
        at = pl.ds(pl.multiple_of(step * 32, 32), 32)
        near, far = iota((32, BOX), 0) + step * 32, iota((32, BOX), 1)
        tz_hi[at, :], tz_lo[at, :] = split(cosines(length_z, near, far))
        ty_hi[at, :], ty_lo[at, :] = split(cosines(jnp.int32(BOX), far, near))
        greet(8 + step * 3, 3)
        return carry

    lax.fori_loop(0, 8, first_tables, 0)
    load_now.wait()
    load_prev.wait()
    block = 32
    groups = lax.div(iota((block, 128), 1), 8)

    def gather_faces(step, carry):
        at = pl.ds(pl.multiple_of(step * block, block), block)
        along_y = (iota((block, BOX), 0) + step * block).astype(F32) * (HALF_PI / BOX)
        along_y = along_y * along_y
        message = jnp.zeros((block, 128), F32)
        for a in range(ROWS):
            wave = pencil * ROWS + a
            along_x = row_of(wave) * HALF_PI / row_of(length_x)
            live = live_z * (jnp.full((1, BOX), wave) < length_x).astype(F32)
            t = along_y + (along_z + along_x * along_x)
            gain = poly(GAIN, t)
            twice_cos = 2.0 - t * gain
            here = m0[a, at, :]
            ahead = live * (twice_cos * here - m_old[a, at, :])
            pushed[a, at, :] = live * gain
            twice[a, at, :] = twice_cos
            free[a, at, :] = ahead
            base = live * (twice_cos * ahead - here)
            mid_hi[a, at, :], mid_lo[a, at, :] = split(dot3(split(base), (tz_hi[...], tz_lo[...])))
            for u, value in enumerate((here, ahead)):
                faces = dot3(split(value), (face_hi, face_lo))
                message = jnp.where(groups == u * ROWS + a, faces, message)
        sent[at, :] = message
        greet(32 + step * 4, 4)
        return carry

    lax.fori_loop(0, BOX // block, gather_faces, 0)
    top = iota((32, 8, BOX), 1) < 4

    def weave(first, second):
        upper = top[:, :, : first.shape[2]]
        even = jnp.where(upper, first, pltpu.roll(second, 4, 1))
        return even, jnp.where(upper, pltpu.roll(first, 4, 1), second)

    for pair in range(2):
        planes = [
            dot3((ty_hi[...], ty_lo[...]), (mid_hi[a], mid_lo[a])).reshape(32, 8, BOX)
            for a in (2 * pair, 2 * pair + 1)
        ]
        for parity, woven in enumerate(weave(*planes)):
            for side in range(2):
                turn[side, pair, :, parity] = woven[:, :, 128 * side : 128 * side + 128]
    pl.semaphore_wait(barrier, EVERYONE - 1)
    pltpu.make_async_copy(sent.at[pl.ds(me, 1)], got.at[pl.ds(me, 1)], own_sem.at[0]).start()
    send_own(sent, got, 0)
    send_rows(sent, got, 0, 1, 7)
    own_turn = pltpu.make_async_copy(turn_of(pencil), pieces_of(pencil), own_sem.at[2])
    own_turn.start()
    bulk_one, bulk_two, bulk_three, bulk_four = BULK
    bulk_after_one = 1 + DOMS * ROWS * bulk_one
    bulk_after_two = bulk_after_one + DOMS * 2 * bulk_two
    bulk_after_three = bulk_after_two + bulk_three
    bulk_after_four = bulk_after_three + 8 * bulk_four

    def x_tables(step, carry):
        send_rows(sent, got, 0, 8 + step * 3, 3)
        send_turn(turn_of, pieces_of, 2, 1 + step * bulk_one, bulk_one)
        part, a = lax.div(step, ROWS), lax.rem(step, ROWS)
        at = pl.ds(pl.multiple_of(a * PENCILS, PENCILS), PENCILS)
        high, low = split(
            cosines(ext[0, part], iota((PENCILS, BOX), 0) * ROWS + a, iota((PENCILS, BOX), 1))
        )
        tx_hi[part, at, :] = high
        tx_lo[part, at, :] = low
        return carry

    lax.fori_loop(0, DOMS * ROWS, x_tables, 0)

    def responses(step, carry):
        send_rows(sent, got, 0, 56 + step, 1)
        send_turn(turn_of, pieces_of, 2, bulk_after_one + step * bulk_two, bulk_two)
        part, half = lax.div(step, 2), lax.rem(step, 2)
        long_x, long_z = ext[0, part], ext[1, part]
        slot = iota((8, BOX), 0)
        rows = jnp.where(slot < 6, cosines(long_z, iota((8, BOX), 1), slot_cells(long_z, slot)), 0.0)
        pairs = jnp.concatenate([rows * rows[i : i + 1] for i in range(8)], axis=0)
        order = iota((128, BOX), 0) + half * 128
        waves = lax.rem(order, PENCILS) * ROWS + lax.div(order, PENCILS)
        along_x = waves.astype(F32) * HALF_PI / row_of(long_x)
        across = waves_z.astype(F32) * HALF_PI / row_of(long_z)
        along_y = row_of(me) * (HALF_PI / BOX)
        gain = poly(GAIN, along_x * along_x + (across * across + along_y * along_y))
        gain = jnp.where((waves < long_x) & (iota((128, BOX), 1) < long_z), gain, 0.0)
        response[part, half] = dot3(split(pairs), split(gain), 1, 1)
        return carry

    lax.fori_loop(0, DOMS * 2, responses, 0)

    def of_strip(strip_index, field):
        value = jnp.zeros_like(strip_index)
        for e in range(STRIPS):
            value = jnp.where(strip_index == e, strips[e, field], value)
        return value

    wide = iota((8 * STRIPS, 32), 0)
    index, depth = lax.div(wide, 8), lax.rem(wide, 8)
    column = iota((8 * STRIPS, 32), 1)
    part, slot = lax.div(column, 8), lax.rem(column, 8)
    face = of_strip(index, 2)

    def weights(parts, side):
        other = slot - 3 * side
        reach = depth + other
        value = jnp.where(reach == 0, 0.25 * COUPLING[0], jnp.where(reach == 1, 0.25 * COUPLING[1], 0.25 * COUPLING[2]))
        hit = (parts == part) & (other >= 0) & (other < 3) & (depth < 3) & (reach < 3)
        return jnp.where(hit, value, 0.0)

    takes = split(jnp.concatenate([weights(of_strip(index, 1), 1 - face), weights(of_strip(index, 0), face)], axis=0))
    tall = iota((32, 8 * STRIPS), 1)
    index, depth = lax.div(tall, 8), lax.rem(tall, 8)
    column = iota((32, 8 * STRIPS), 0)
    part, slot = lax.div(column, 8), lax.rem(column, 8)
    gives = (part == of_strip(index, 0)) & (slot == 3 * of_strip(index, 2) + depth) & (depth < 3)
    gives = jnp.where(gives, 1.0, 0.0).astype(BF16)
    index = lax.div(iota((8 * STRIPS, BOX), 0), 8)
    cells = iota((8 * STRIPS, BOX), 1)
    start = of_strip(index, 3)
    inside = (cells >= start) & (cells < start + of_strip(index, 5))

    def force(face_modes):
        faces = jnp.concatenate(
            [dot_thin(face_modes[p], (tx_hi[p], tx_lo[p]), 0) for p in range(DOMS)], axis=0
        )
        taken = dot3(takes, split(faces))
        shifted = [
            pltpu.roll(taken[8 * e : 8 * e + 8], lax.rem(strips[e, 3] - strips[e, 4] + BOX, BOX), 1)
            for e in range(STRIPS)
        ]
        gap = split(jnp.where(inside, jnp.concatenate(shifted, axis=0) - taken[8 * STRIPS :], 0.0))
        forcing = dot(gives, gap[0], 1, 0) + dot(gives, gap[1], 1, 0)
        return [dot_thin(forcing[8 * p : 8 * p + 8], (tx_hi[p], tx_lo[p]), 1) for p in range(DOMS)]

    send_turn(turn_of, pieces_of, 2, bulk_after_two, bulk_three)
    wait_rows(sent, got, 0)
    first, second = [], []
    for pair in range(2):
        turned = got[128 * pair : 128 * pair + 128, :].T
        for p in range(2):
            for u, held in enumerate((first, second)):
                held.append(
                    jnp.concatenate(
                        [
                            turned[8 * (u * ROWS + a) : 8 * (u * ROWS + a) + 8, PENCILS * p : PENCILS * (p + 1)]
                            for a in range(ROWS)
                        ],
                        axis=1,
                    )
                )
    force_one = force(first)
    answered = []
    for p in range(DOMS):
        both = jnp.concatenate([response[p, 0], response[p, 1]], axis=1).reshape(8, 8, BOX)
        answered.append(second[p] + jnp.sum(both * force_one[p][None], axis=1))
    force_two = force(answered)
    for pair in range(2):
        rows = [
            jnp.concatenate(
                [forces[2 * pair + p][:, PENCILS * a : PENCILS * (a + 1)] for p in range(2)], axis=1
            )
            for forces in (force_one, force_two)
            for a in range(ROWS)
        ]
        rows.append(jnp.zeros((64, 128), F32))
        back[128 * pair : 128 * pair + 128, :] = jnp.concatenate(rows, axis=0).T
    pltpu.make_async_copy(back.at[pl.ds(me, 1)], returned.at[pl.ds(me, 1)], own_sem.at[1]).start()
    send_own(back, returned, 1)
    send_rows(back, returned, 1, 1, 7)

    chunk = iota((1, 128), 1)
    later, power = lax.div(chunk, 64), lax.rem(lax.div(chunk, 8), 8)
    rows_of = []
    for m in range(8):
        row = jnp.zeros((1, 128), F32)
        for u, coefs in enumerate((PUSHED_GAIN, GAIN)):
            for j in range(len(coefs) - m):
                coef = coefs[m + j] * math.comb(m + j, j) * MID**j
                row = jnp.where((later == u) & (power == j), coef, row)
        rows_of.append(row)

    def late_tables(step, carry):
        send_rows(back, returned, 1, 8 + step * 7, 7)
        send_turn(turn_of, pieces_of, 2, bulk_after_three + step * bulk_four, bulk_four)
        at = pl.ds(pl.multiple_of(step * 32, 32), 32)
        rows = iota((128, BOX), 0)
        cells = lax.rem(rows, 8)
        values = cosines(length_z, iota((128, BOX), 1), slot_cells(length_z, cells))
        values = jnp.where((cells < 6) & (lax.div(rows, 8) == step), values, 0.0)
        edge_hi[step], edge_lo[step] = split(values)
        order = iota((32, BOX), 1)
        waves = lax.rem(order, PENCILS) * ROWS + lax.div(order, PENCILS)
        xt_hi[at, :], xt_lo[at, :] = split(cosines(length_x, waves, iota((32, BOX), 0) + step * 32))
        along_y = (iota((32, 128), 0) + step * 32).astype(F32) * (HALF_PI / BOX)
        along_y = along_y * along_y + MID
        for a in range(ROWS):
            wave = pencil * ROWS + a
            along_x = row_of(wave) * HALF_PI / row_of(length_x)
            t = along_y + (along_x * along_x)[:, :128]
            value = rows_of[7] * t + rows_of[6]
            for m in range(5, -1, -1):
                value = value * t + rows_of[m]
            lift[a, at, :] = jnp.where(jnp.full((1, 128), wave) < length_x, value, 0.0)
        return carry

    lax.fori_loop(0, 8, late_tables, 0)
    send_turn(turn_of, pieces_of, 2, bulk_after_four, PENCILS - bulk_after_four)
    rows = iota((64, BOX), 0)
    cells = lax.rem(rows, 8)
    values = jnp.where(cells < 6, cosines(length_z, iota((64, BOX), 1), slot_cells(length_z, cells)), 0.0)
    offset = along_z * (1.0 / MID) - 1.0
    raised, factor = jnp.ones_like(values), jnp.broadcast_to(offset, (64, BOX))
    for j in range(1, 8):
        raised = jnp.where(lax.div(rows, 8) >= j, raised * factor, raised)
    spread = dot3(split(values * raised), (tz_hi[...], tz_lo[...]))
    nothing = jnp.zeros_like(spread)
    for a in range(2):
        zt_hi[a], zt_lo[a] = split(jnp.concatenate([nothing, spread] if a else [spread, nothing], axis=0))

    wait_rows(back, returned, 1)
    come = split(returned[...])
    source, goal = iota((128, 128), 0), iota((128, 128), 1)
    half = iota((BOX, 128), 1) < 64
    planes = []
    for pair in range(2):
        lifted = []
        for a in (2 * pair, 2 * pair + 1):
            pick = (source == lax.div(goal, 64) * (8 * ROWS) + 8 * a + lax.rem(goal, 8)).astype(F32).astype(BF16)
            value = (dot(come[0], pick, 1, 0) + dot(come[1], pick, 1, 0)) * lift[a]
            lifted.append(value + pltpu.roll(value, 64, 1))
        plane = dot3((ty_hi[...], ty_lo[...]), split(jnp.where(half, lifted[0], lifted[1])))
        planes.append(plane.reshape(32, 8, 128))
    for parity, woven in enumerate(weave(*planes)):
        late_turn[:, parity] = woven
    own_late = pltpu.make_async_copy(late_turn_of(pencil), late_of(pencil), own_sem.at[3])
    own_late.start()

    def send_late(step, carry):
        send_turn(late_turn_of, late_of, 3, 1 + step * 9, 9)
        return carry

    lax.fori_loop(0, 7, send_late, 0)
    for a in range(ROWS):
        live = live_z * (jnp.full((1, BOX), pencil * ROWS + a) < length_x).astype(F32)
        for piece in range(2):
            at = slice(128 * piece, 128 * piece + 128)
            left = (come[0][at], come[1][at])
            gain = pushed[a, at, :]
            m1 = free[a, at, :] + gain * dot3(left, (edge_hi[a], edge_lo[a]))
            one_out[a, at, :] = m1
            two_out[a, at, :] = live * (twice[a, at, :] * m1 - m0[a, at, :]) + gain * dot3(
                left, (edge_hi[ROWS + a], edge_lo[ROWS + a])
            )
    own_turn.wait()
    own_late.wait()
    pltpu.make_async_remote_copy(
        src_ref=pieces.at[:, :, pl.ds(0, PENCILS - 1)],
        dst_ref=pieces.at[:, :, pl.ds(0, PENCILS - 1)],
        send_sem=send_sem.at[2],
        recv_sem=recv_sem.at[2],
        device_id=(dom, lax.rem(pencil + 1, PENCILS)),
        device_id_type=MESH,
    ).wait()
    pltpu.make_async_remote_copy(
        src_ref=late.at[pl.ds(0, PENCILS - 1)],
        dst_ref=late.at[pl.ds(0, PENCILS - 1)],
        send_sem=send_sem.at[3],
        recv_sem=recv_sem.at[3],
        device_id=(dom, lax.rem(pencil + 1, PENCILS)),
        device_id_type=MESH,
    ).wait()


def spread_kernel(pieces, late, xt_hi, xt_lo, zt_hi, zt_lo, one, two, one_out, two_out, pressure, held, sems):
    copies = [
        pltpu.make_async_copy(one, one_out, sems.at[0]),
        pltpu.make_async_copy(two, two_out, sems.at[1]),
    ]
    for copy in copies:
        copy.start()
    fields = []
    for y in range(ROWS):
        rows = [late[pl.ds(ROWS * pair + y, PENCILS, stride=8), :] for pair in range(2)]
        rows = split(jnp.concatenate(rows, axis=0))
        extra = [dot3(rows, (zt_hi[a], zt_lo[a])) for a in range(2)]
        parts = []
        for a in range(ROWS):
            pair, odd = a // 2, a % 2
            sides = [
                pieces[pl.ds(side * BOX * ROWS + pair * 8 * PENCILS + odd * ROWS + y, PENCILS, stride=8), :]
                for side in range(2)
            ]
            parts.append(jnp.concatenate(sides, axis=1) + extra[odd][PENCILS * pair : PENCILS * (pair + 1)])
        fields.append(split(jnp.concatenate(parts, axis=0)))
    for part in range(PARTS):
        at = slice(part * (BOX // PARTS), (part + 1) * (BOX // PARTS))
        table = (xt_hi[at, :], xt_lo[at, :])
        for y in range(ROWS):
            held[at, y, :] = dot3(table, fields[y])
        copy = pltpu.make_async_copy(held.at[at], pressure.at[at], sems.at[2 + part])
        copy.start()
        copies.append(copy)
    for copy in copies:
        copy.wait()


def on_device(modes_now, modes_prev, extents, strips):
    vmem, hbm, anywhere = (
        pl.BlockSpec(memory_space=space) for space in (pltpu.VMEM, pltpu.HBM, pl.ANY)
    )
    field = jax.ShapeDtypeStruct((ROWS, BOX, BOX), F32)
    half_table = jax.ShapeDtypeStruct((BOX, BOX), BF16)
    wide_table = jax.ShapeDtypeStruct((2, 128, BOX), BF16)
    one, two, pieces, late, xt_hi, xt_lo, zt_hi, zt_lo = pl.pallas_call(
        coupled_kernel,
        out_shape=(
            field,
            field,
            jax.ShapeDtypeStruct((2, 2, PENCILS, 8, 128), F32),
            jax.ShapeDtypeStruct((PENCILS, 8, 128), F32),
            half_table,
            half_table,
            wide_table,
            wide_table,
        ),
        in_specs=[hbm] * 4,
        out_specs=[vmem] * 8,
        scratch_shapes=[pltpu.VMEM((ROWS, BOX, BOX), F32)] * 5
        + [pltpu.VMEM((EVERYONE, 128), F32)] * 4
        + [pltpu.VMEM((DOMS, BOX, BOX), BF16)] * 2
        + [pltpu.VMEM((DOMS, 2, 64, 128), F32)]
        + [pltpu.VMEM((2 * ROWS, 128, BOX), BF16)] * 2
        + [pltpu.VMEM((BOX, BOX), BF16)] * 4
        + [pltpu.VMEM((ROWS, BOX, BOX), BF16)] * 2
        + [pltpu.VMEM((2, 2, PENCILS // 2, 2, 8, 128), F32)]
        + [pltpu.VMEM((ROWS, BOX, 128), F32), pltpu.VMEM((PENCILS // 2, 2, 8, 128), F32)]
        + [pltpu.SMEM((2, DOMS), I32), pltpu.SMEM((STRIPS, 6), I32)]
        + [pltpu.SemaphoreType.DMA((4,))] * 4,
        compiler_params=pltpu.CompilerParams(has_side_effects=True, collective_id=1, vmem_limit_bytes=199 << 18),
        name="coupled",
    )(extents.T, strips, modes_now[0], modes_prev[0])
    one, two, pressure = pl.pallas_call(
        spread_kernel,
        out_shape=(field, field, jax.ShapeDtypeStruct((BOX, ROWS, BOX), F32)),
        in_specs=[vmem] * 8,
        out_specs=[anywhere] * 3,
        scratch_shapes=[pltpu.VMEM((BOX, ROWS, BOX), F32), pltpu.SemaphoreType.DMA((2 + PARTS,))],
        compiler_params=pltpu.CompilerParams(vmem_limit_bytes=24 << 20),
        name="spread",
    )(pieces.reshape(2 * BOX * ROWS, 128), late.reshape(PENCILS * 8, 128), xt_hi, xt_lo, zt_hi, zt_lo, one, two)
    return (two[None], one[None], pressure[None])


def solution(mesh):
    return jax.shard_map(
        on_device,
        mesh=mesh,
        in_specs=(P("dom", "pencil", None, None), P("dom", "pencil", None, None), P(), P()),
        out_specs=(
            P("dom", "pencil", None, None),
            P("dom", "pencil", None, None),
            P("dom", None, "pencil", None),
        ),
        check_vma=False,
    )
```
